32 devices in a mesh: grp: 8 (over z, x), rep: 4 (over y, core).
Axes of the slice: x: 2, y: 2, z: 4, core: 2. Of those that a mesh axis runs over, the one named last changes fastest.
Arguments:
- strain: bfloat16 [1280, 384], P(None, 'grp'), may hold values from -27 to 27
- fir_taps: float32 [64], replicated, may hold values from -0.75 to 0.75
- half_widths: int32 [1280], P('grp'), may hold values from 32 to 160
- pairs: int32 [32, 8], replicated, may hold values from -1 to 31, as said below
Outputs:
- correlations: bfloat16 [32, 8, 40, 40, 256], P(('grp', 'rep'))
The draws below stay inside these ranges and needn't reach their ends.
Inputs may be any that keep to these rules, and one draw needn't show every extreme that they name: `pairs`: row e lists tile numbers; -1 marks an unused entry and used entries come first; no two used entries of a row lie in the same group of 4 consecutive tiles, none equals e; every row has a used entry and some row uses all 8.
All inputs are finite; a program needn't handle non-finite values.
Results may differ from the reference program's by a relative error of at most 0.0052.
Values may be sent and summed in bfloat16 or wider, within the bound.
No kernel may reach another device: no remote copies, remote signals or barrier semaphores. Data moves between devices by JAX's collectives and lax.ppermute only.
A program may use at most 128 MiB of HBM per device.

```python
import math
import jax
import jax.numpy as jnp
from jax import lax

TILE = 40
NT = 384
LAGS = 256
TAPS = 64
PMAX = 8
TILES = 32
CH = 1280
N_GRP = 8
N_REP = 4


def draw_strain(key, part):
    key = jax.random.fold_in(key, 5)
    key_base, key_level = jax.random.split(key)
    base = jnp.clip(jax.random.normal(key_base, (CH, NT), jnp.float32), -6.0, 6.0)
    level = jax.random.uniform(key_level, (CH, NT // 32, 1), jnp.float32, -1.5, 1.5)
    envelope = jnp.broadcast_to(jnp.exp(level), (CH, NT // 32, 32)).reshape(CH, NT)
    return (base * envelope).astype(jnp.bfloat16)


def draw_pairs(key, part):
    key = jax.random.fold_in(key, 11)
    key_rows, key_reps, key_counts, key_heavy, key_full = jax.random.split(key, 5)
    row_keys = jax.random.split(key_rows, TILES)
    groups = jax.vmap(lambda item: jax.random.permutation(item, N_GRP))(row_keys)[:, :PMAX].astype(jnp.int32)
    members = jax.random.randint(key_reps, (TILES, PMAX), 0, N_REP, dtype=jnp.int32)
    tile_ids = jnp.arange(TILES, dtype=jnp.int32)
    slots = jnp.arange(PMAX, dtype=jnp.int32)[None, :]
    full_row = jax.random.randint(key_full, (), 0, N_REP, dtype=jnp.int32)
    is_full = (tile_ids == full_row)[:, None]
    groups = jnp.where(is_full, N_GRP - 1 - slots, groups)
    members = jnp.where(is_full & (slots == 0), N_REP - 1, members)
    own_group = (tile_ids // N_REP)[:, None]
    own_member = (tile_ids % N_REP)[:, None]
    members = jnp.where((groups == own_group) & (members == own_member), (members + 1) % N_REP, members)
    light_counts = jax.random.randint(key_counts, (TILES,), 1, PMAX // 2 + 1, dtype=jnp.int32)
    heavy_rows = jax.random.randint(key_heavy, (TILES,), 0, 4, dtype=jnp.int32) == 0
    counts = jnp.where(heavy_rows | (tile_ids == full_row), PMAX, light_counts)
    listed = groups * N_REP + members
    return jnp.where(slots < counts[:, None], listed, -1).astype(jnp.int32)


def set_ends(values, rng, smallest, high):
    shape = values.shape
    place = [jax.random.randint(jax.random.fold_in(rng, axis), (), 0, shape[axis]) for axis in range(len(shape))]
    values = values.at[tuple(place)].set(smallest)
    longest = shape.index(max(shape))
    place[longest] = (place[longest] + 1) % shape[longest]
    return values.at[tuple(place)].set(high)


def bell_draw(own_key, shape, spread, reach, held_as=jnp.bfloat16):
    drawn = spread * jax.random.normal(own_key, shape, jnp.float32)
    return jnp.clip(drawn, min=-reach, max=reach).astype(held_as)


def setup_inputs(seed: int = 0) -> dict:
    seeds = jax.random.split(jax.random.key(seed), 5)
    return {
        "strain": draw_strain(jax.random.fold_in(seeds[4], 71), 0),
        "fir_taps": bell_draw(seeds[1], (TAPS,), TAPS ** -0.5, 0.75, jnp.float32),
        "half_widths": set_ends(jax.random.randint(seeds[2], (CH,), 32, 161), jax.random.fold_in(seeds[2], 1), 32, 160).astype(jnp.int32),
        "pairs": draw_pairs(jax.random.fold_in(seeds[4], 71), 0),
    }


def band_filter(samples, fir_taps):
    channels, length = samples.shape
    blocks = length // 128
    count = fir_taps.shape[0]
    rows_at = jnp.arange(128, dtype=jnp.int32)[:, None]
    cols_at = jnp.arange(128, dtype=jnp.int32)[None, :]
    tap_ids = jnp.arange(count, dtype=jnp.int32)
    near_gap = cols_at - rows_at
    far_gap = near_gap + 128
    taps_near = lax.optimization_barrier(jnp.sum(jnp.where(near_gap[:, :, None] == tap_ids, fir_taps, jnp.float32(0.0)), axis=2))
    taps_far = lax.optimization_barrier(jnp.sum(jnp.where(far_gap[:, :, None] == tap_ids, fir_taps, jnp.float32(0.0)), axis=2))
    blocked = samples.reshape(channels, blocks, 128)
    previous = jnp.concatenate([jnp.zeros((channels, 1, 128), jnp.float32), blocked[:, :-1]], axis=1)
    result = jnp.einsum('cbs,st->cbt', blocked, taps_near, precision=lax.Precision.HIGHEST)
    result = result + jnp.einsum('cbs,st->cbt', previous, taps_far, precision=lax.Precision.HIGHEST)
    return result.reshape(channels, length)

def normalize(filtered, widths):
    channels, length = filtered.shape
    running = jnp.cumsum(jnp.abs(filtered), axis=1)
    prefix = jnp.concatenate([jnp.zeros((channels, 1), jnp.float32), running], axis=1)
    steps = jnp.arange(length, dtype=jnp.int32)[None, :]
    upper_end = jnp.minimum(steps + widths[:, None], length - 1) + 1
    lower_end = jnp.maximum(steps - widths[:, None], 0)
    window_sum = jnp.take_along_axis(prefix, upper_end.astype(jnp.int32), axis=1) - jnp.take_along_axis(prefix, lower_end.astype(jnp.int32), axis=1)
    level = window_sum / (2.0 * widths[:, None].astype(jnp.float32) + 1.0)
    return (filtered / (level + 1e-05)).astype(jnp.bfloat16)

def condition(samples, fir_taps, widths):
    return normalize(band_filter(samples.astype(jnp.float32), fir_taps), widths)

def lag_matrix(own, first, count, summed):
    length = own.shape[1]
    positions = jnp.arange(length, dtype=jnp.int32)[None, :]
    shifts = first + jnp.arange(count, dtype=jnp.int32)[:, None]
    offsets = positions - shifts
    inside = (offsets >= 0) & (offsets < summed)
    picked = own[:, jnp.clip(offsets, 0, length - 1)]
    return jnp.where(inside[None], picked, jnp.zeros((), own.dtype))

def reference(strain, fir_taps, half_widths, pairs):
    whitened = condition(strain, fir_taps, half_widths)
    tiles = whitened.reshape(TILES, TILE, NT)
    summed = NT - LAGS
    normalizer = 1.0 / math.sqrt(summed)

    def one_tile(inputs):
        own, listed = inputs
        partner = jnp.take(tiles, jnp.clip(listed, 0, TILES - 1), axis=0).astype(jnp.float32)
        partner = jnp.where((listed >= 0)[:, None, None], partner, jnp.float32(0.0))
        shifted = lag_matrix(own, 0, LAGS, summed).astype(jnp.float32)
        product = jnp.einsum('pju,ilu->pjil', partner, shifted, precision=lax.Precision.HIGHEST)
        return (product * normalizer).astype(jnp.bfloat16)
    return lax.map(one_tile, (tiles, pairs))
```

```python
import functools
import math

import jax
import jax.numpy as jnp
from jax import lax
from jax.experimental import pallas as pl
from jax.experimental.pallas import tpu as pltpu
from jax.sharding import PartitionSpec as P

TILE = 40
LAGS = 256
LANES = 128
PER_BLOCK = LANES // TILE
CHUNK = 2


def pack_kernel(rep_count, pairs_ref, strain_ref, widths_ref, out_ref, blocks_ref, table_ref):
    groups, rows, packed = out_ref.shape
    listed = pairs_ref.shape[0]
    channels = strain_ref.shape[1]
    members = widths_ref.shape[1]
    my_rep = lax.axis_index("rep")
    my_grp = lax.axis_index("grp")

    count = channels // LANES
    for block in range(count):
        blocks_ref[block] = strain_ref[:, block * LANES : (block + 1) * LANES].astype(jnp.float32)
    blocks_ref[count] = jnp.zeros((rows, LANES), jnp.float32)

    wide = jnp.concatenate(
        [widths_ref[...].astype(jnp.float32), jnp.zeros((1, 2 * LANES - members), jnp.float32)],
        axis=1,
    )
    wide = jnp.broadcast_to(wide, (8, 2 * LANES))
    sub = lax.broadcasted_iota(jnp.int32, (8, LANES), 0)
    spare = LANES - 8
    for member in range(rep_count):
        for block in range(packed // LANES):
            runs = []
            for line in range(2):
                run = (line * (packed // LANES) + block) * 8
                shift = (spare - member * TILE - run) % (2 * LANES)
                runs.append(pltpu.roll(wide, shift, 1)[:, :LANES])
            even = lax.rem(sub, 2) == 0
            table_ref[member, :, block * LANES : (block + 1) * LANES] = jnp.where(even, runs[0], runs[1])

    lane = lax.broadcasted_iota(jnp.int32, (rows, LANES), 1)
    row = lax.broadcasted_iota(jnp.int32, (rows, LANES), 0)

    def fill(group, carry):
        tile = group * rep_count + my_rep
        chosen = [tile]
        member = jnp.int32(0)
        for slot in range(listed):
            other = pairs_ref[slot, tile]
            chosen.append(jnp.maximum(other, 0))
            inside = (other >= 0) & (lax.div(other, rep_count) == my_grp)
            member = jnp.where(inside, lax.rem(other, rep_count), member)
        for block in range(packed // LANES):
            total = jnp.zeros((rows, LANES), jnp.float32)
            for place in range(PER_BLOCK):
                index = block * PER_BLOCK + place
                if index > listed:
                    continue
                start = chosen[index] * TILE
                source = lax.div(start, LANES)
                offset = lax.rem(start, LANES)
                both = jnp.where(lane >= offset, blocks_ref[source], blocks_ref[source + 1])
                shift = lax.rem(place * TILE + LANES - offset, LANES)
                moved = pltpu.roll(both, shift, 1)
                here = (lane >= place * TILE) & (lane < (place + 1) * TILE)
                total = jnp.where(here, moved, total)
            at = pl.ds(block * LANES, LANES)
            theirs = table_ref[member, :, at]
            mine = table_ref[my_rep, :, at]
            short = min(rows, 8)
            top_row = row[:short]
            extra = jnp.where(top_row < 2, theirs[:short], mine[:short])
            marked = (lane[:short] >= spare) & (top_row < 4)
            top = jnp.where(marked, extra, total[:short])
            if rows > 8:
                total = jnp.concatenate([top, total[8:]], axis=0)
            else:
                total = top
            out_ref[group, :, at] = total.astype(jnp.bfloat16)
        return carry

    lax.fori_loop(0, groups, fill, 0)


def pack(strain, half_widths, pairs, groups, rep_count):
    channels, rows = strain.shape
    listed = pairs.shape[1]
    packed = -(-(listed + 1) // PER_BLOCK) * LANES
    vmem = pl.BlockSpec(memory_space=pltpu.VMEM)
    return pl.pallas_call(
        functools.partial(pack_kernel, rep_count),
        out_shape=jax.ShapeDtypeStruct((groups, rows, packed), jnp.bfloat16),
        in_specs=[pl.BlockSpec(memory_space=pltpu.SMEM), vmem, vmem],
        out_specs=vmem,
        scratch_shapes=[
            pltpu.VMEM((channels // LANES + 1, rows, LANES), jnp.float32),
            pltpu.VMEM((rep_count, 8, packed), jnp.float32),
        ],
        compiler_params=pltpu.CompilerParams(vmem_limit_bytes=48 * 2**20),
        name="pack",
    )(pairs.T, strain.T, half_widths[None, :])


def split(values):
    high = values.astype(jnp.bfloat16)
    low = (values - high.astype(jnp.float32)).astype(jnp.bfloat16)
    return high, low


def dot(left, right):
    return jnp.dot(left, right, preferred_element_type=jnp.float32)


def condition(rep_count, pairs_ref, raw_ref, taps_ref, tops_ref, white_ref):
    length, packed = raw_ref.shape
    listed = pairs_ref.shape[0]
    groups = lax.axis_size("grp")
    rows = length // groups
    my_rep = lax.axis_index("rep")
    my_grp = lax.axis_index("grp")
    tile = my_grp * rep_count + my_rep

    raw = raw_ref[...]
    raw32 = raw.astype(jnp.float32)
    short = min(rows, 8)
    for group in range(groups):
        tops_ref[group, :short] = raw32[group * rows : group * rows + short]
    samples = jnp.transpose(raw32).astype(jnp.bfloat16)

    count = taps_ref.shape[1]
    taps = jnp.concatenate([taps_ref[...], jnp.zeros((1, 2 * LANES - count), jnp.float32)], axis=1)
    band = pltpu.roll(jnp.broadcast_to(taps, (LANES, 2 * LANES)), 0, 1, stride=1, stride_axis=0)
    parts = []
    empty = jnp.zeros((LANES, LANES), jnp.bfloat16)
    for piece in split(band):
        near, far = piece[:, :LANES], piece[:, LANES:]
        first = jnp.concatenate([piece, jnp.concatenate([empty, near], axis=1)], axis=0)
        second = jnp.concatenate([far, near], axis=0)
        parts.append((dot(samples[:, : 2 * LANES], first), dot(samples[:, LANES:], second)))
    filtered = jnp.concatenate([parts[0][0] + parts[1][0], parts[0][1] + parts[1][1]], axis=1)

    size = jnp.abs(filtered)
    before = lax.broadcasted_iota(jnp.int32, (2 * LANES, 2 * LANES), 0) <= lax.broadcasted_iota(
        jnp.int32, (2 * LANES, 2 * LANES), 1
    )
    upper = jnp.where(before, 1.0, 0.0).astype(jnp.bfloat16)
    ones = jnp.ones((2 * LANES, LANES), jnp.bfloat16)
    sums = []
    for piece in split(size):
        head, tail = piece[:, : 2 * LANES], piece[:, 2 * LANES :]
        sums.append((dot(head, upper), dot(head, ones), dot(tail, upper[:LANES, :LANES])))
    high, low = sums
    head = high[0] + low[0]
    tail = (high[1] + low[1]) + (high[2] + low[2])
    prefix = [head[:, :LANES], head[:, LANES:], tail]

    lane8 = lax.broadcasted_iota(jnp.int32, (8, LANES), 1)
    sub8 = lax.broadcasted_iota(jnp.int32, (8, LANES), 0)
    lane = lax.broadcasted_iota(jnp.int32, (TILE, LANES), 1)
    blocks = packed // LANES
    for slot in range(listed + 1):
        base = slot // PER_BLOCK * LANES + slot % PER_BLOCK * TILE
        at = slice(base, base + TILE)
        if slot == 0:
            source, line = my_grp, 2
            used = None
        else:
            other = pairs_ref[slot - 1, tile]
            source, line = lax.div(jnp.maximum(other, 0), rep_count), 0
            used = other >= 0
        widths = []
        for run in range(TILE // 8):
            lanes = pl.ds(run % blocks * LANES, LANES)
            at_line = pl.ds(line + run // blocks, 1)
            shown = jnp.broadcast_to(tops_ref[source, at_line, lanes], (8, LANES))
            picked = jnp.where(lane8 == sub8 + (LANES - 8), shown, 0.0)
            widths.append(jnp.sum(picked, axis=1, keepdims=True))
        width = jnp.broadcast_to(jnp.concatenate(widths, axis=0), (TILE, LANES))
        whole = width.astype(jnp.int32)
        above = lane + whole
        below = lane - whole - 1
        above_at = above & (LANES - 1)
        below_at = below & (LANES - 1)
        above_by = above >> 7
        below_by = below >> 7
        up = [jnp.take_along_axis(prefix[b][at], above_at, axis=1) for b in range(3)]
        down = [jnp.take_along_axis(prefix[b][at], below_at, axis=1) for b in range(2)]
        full = jnp.broadcast_to(prefix[2][at][:, LANES - 1 :], (TILE, LANES))
        ends = up + [full, full]
        starts = [jnp.zeros((TILE, LANES), jnp.float32)] * 2 + down
        down_last = jnp.take_along_axis(prefix[2][at], below_at, axis=1)
        starts.append(down_last)
        scale = 2.0 * width + 1.0
        for block in range(3):
            top = jnp.where(above_by == 0, ends[block], jnp.where(above_by == 1, ends[block + 1], ends[block + 2]))
            low_end = jnp.where(
                below_by == 0,
                starts[block + 2],
                jnp.where(below_by == -1, starts[block + 1], starts[block]),
            )
            level = (top - low_end) / scale
            value = filtered[at, block * LANES : (block + 1) * LANES] / (level + 1e-05)
            if used is not None:
                value = jnp.where(used, value, 0.0)
            white_ref[slot * TILE : (slot + 1) * TILE, block * LANES : (block + 1) * LANES] = value


def lag_weights(white_ref, weights_ref):
    own = white_ref[:TILE, :LANES].astype(jnp.bfloat16)
    row = lax.broadcasted_iota(jnp.int32, (LANES, LANES), 0)
    col = lax.broadcasted_iota(jnp.int32, (LANES, LANES), 1)
    flip = jnp.where(row + col == LANES - 1, 1.0, 0.0).astype(jnp.bfloat16)
    reverse = dot(own, flip)
    keep = col <= row
    for channel in range(TILE):
        line = jnp.broadcast_to(reverse[channel : channel + 1], (LANES, LANES))
        turned = pltpu.roll(line, 1, 1, stride=1, stride_axis=0)
        first = jnp.where(keep, turned, 0.0).astype(jnp.bfloat16)
        second = jnp.where(keep, 0.0, turned).astype(jnp.bfloat16)
        at = slice(channel % 2 * LANES, (channel % 2 + 1) * LANES)
        weights_ref[channel // 2, :LANES, at] = first
        weights_ref[channel // 2, LANES:, at] = second


def correlate_kernel(
    rep_count, pairs_ref, raw_ref, taps_ref, out_ref, tops_ref, white_ref, weights_ref, low_ref, high_ref
):
    step = pl.program_id(0)

    @pl.when(step == 0)
    def _():
        condition(rep_count, pairs_ref, raw_ref, taps_ref, tops_ref, white_ref)
        lag_weights(white_ref, weights_ref)

    rows = CHUNK * TILE
    start = pl.multiple_of(TILE + step * rows, 8)
    partner = white_ref[pl.ds(start, rows), :].astype(jnp.bfloat16)
    early = partner[:, : 2 * LANES]
    late = partner[:, LANES:]
    normalizer = 1.0 / math.sqrt(LANES)

    def pair_of_channels(index, carry):
        weights = weights_ref[index]
        for part, ref in ((early, low_ref), (late, high_ref)):
            product = dot(part, weights) * normalizer
            for side in range(2):
                ref[pl.ds(2 * index + side, rows, stride=TILE), :] = product[
                    :, side * LANES : (side + 1) * LANES
                ]
        return carry

    lax.fori_loop(0, TILE // 2, pair_of_channels, 0, unroll=4)

    def finish(index, carry):
        at = pl.ds(pl.multiple_of(index * TILE * TILE, TILE * TILE), TILE * TILE)
        for side, ref in enumerate((low_ref, high_ref)):
            block = ref[at, :].astype(jnp.bfloat16).reshape(TILE, TILE, LANES)
            out_ref[0, index, :, :, side * LANES : (side + 1) * LANES] = block
        return carry

    lax.fori_loop(0, CHUNK, finish, 0)


def correlate(raw, fir_taps, pairs, rep_count):
    length, packed = raw.shape
    listed = pairs.shape[1]
    rows = CHUNK * TILE
    vmem = pl.BlockSpec(memory_space=pltpu.VMEM)
    return pl.pallas_call(
        functools.partial(correlate_kernel, rep_count),
        grid=(listed // CHUNK,),
        out_shape=jax.ShapeDtypeStruct((1, listed, TILE, TILE, LAGS), jnp.bfloat16),
        in_specs=[pl.BlockSpec(memory_space=pltpu.SMEM), vmem, vmem],
        out_specs=pl.BlockSpec((1, CHUNK, TILE, TILE, LAGS), lambda step: (0, step, 0, 0, 0)),
        scratch_shapes=[
            pltpu.VMEM((lax.axis_size("grp"), 8, packed), jnp.float32),
            pltpu.VMEM(((listed + 1) * TILE, length), jnp.float32),
            pltpu.VMEM((TILE // 2, 2 * LANES, 2 * LANES), jnp.bfloat16),
            pltpu.VMEM((rows * TILE, LANES), jnp.float32),
            pltpu.VMEM((rows * TILE, LANES), jnp.float32),
        ],
        compiler_params=pltpu.CompilerParams(vmem_limit_bytes=48 * 2**20),
        name="correlate",
    )(pairs.T, raw, fir_taps[None, :])


def on_device(strain, fir_taps, half_widths, pairs):
    groups = lax.axis_size("grp")
    rep_count = lax.axis_size("rep")
    message = pack(strain, half_widths, pairs, groups, rep_count)
    received = lax.all_to_all(message, "grp", split_axis=0, concat_axis=0, tiled=True)
    raw = received.reshape(-1, received.shape[2])
    return correlate(raw, fir_taps, pairs, rep_count)


def solution(mesh):
    placed = (P(None, "grp"), P(), P("grp"), P())
    return jax.shard_map(
        on_device,
        mesh=mesh,
        in_specs=placed,
        out_specs=P(("grp", "rep"), None, None, None, None),
        check_vma=False,
    )
```

```python
import functools
import math

import jax
import jax.numpy as jnp
from jax import lax
from jax.experimental import pallas as pl
from jax.experimental.pallas import tpu as pltpu
from jax.sharding import PartitionSpec as P

TILE = 40
LAGS = 256
LANES = 128
STRIDE = 9
PER_BLOCK = LANES // TILE


def fetch(pairs, semaphores):
    copies = [
        pltpu.make_async_copy(source, target, semaphores.at[index])
        for index, (source, target) in enumerate(pairs)
    ]
    for copy in copies:
        copy.start()
    for copy in copies:
        copy.wait()


def partner_of(group, step, groups):
    if groups & (groups - 1) == 0:
        return group ^ step
    return (step + groups - group) % groups


def rounds(groups):
    even = list(range(groups - 1, 0, -1))
    far = groups // 2
    odd = [step for step in even if step < far] + [step for step in even if step >= far]
    return list(zip(even, odd)) + [(0, 0)]


def step_of(steps, member):
    even, odd = steps
    return even if even == odd else jnp.where(lax.rem(member, 2) == 0, even, odd)


def pack_kernel(rep_count, pairs_hbm, strain_hbm, widths_hbm, taps_hbm, *refs):
    outs_hbm = refs[:-9]
    taps_ref, stage_ref, sent = refs[-9:-6]
    out_refs = [stage_ref.at[index] for index in range(len(outs_hbm))]
    pairs_ref, strain_ref, widths_ref, semaphores, blocks_ref, table_ref = refs[-6:]
    groups = len(out_refs)
    rows, packed = out_refs[0].shape
    listed = pairs_ref.shape[0]
    channels = strain_ref.shape[1]
    members = widths_ref.shape[1]
    fetch(
        [
            (strain_hbm, strain_ref),
            (pairs_hbm, pairs_ref),
            (widths_hbm, widths_ref),
            (taps_hbm, taps_ref),
        ],
        semaphores,
    )
    my_rep = lax.axis_index("rep")
    my_grp = lax.axis_index("grp")

    count = channels // LANES
    filled = strain_ref.shape[0]
    for block in range(count):
        values = strain_ref[:, block * LANES : (block + 1) * LANES].astype(jnp.float32)
        if rows > filled:
            values = jnp.concatenate([values, jnp.zeros((rows - filled, LANES), jnp.float32)], axis=0)
        blocks_ref[block] = values
    blocks_ref[count] = jnp.zeros((rows, LANES), jnp.float32)

    wide = jnp.concatenate(
        [widths_ref[...].astype(jnp.float32), jnp.zeros((1, 2 * LANES - members), jnp.float32)],
        axis=1,
    )
    wide = jnp.broadcast_to(wide, (TILE, 2 * LANES))
    tall = lax.broadcasted_iota(jnp.int32, (TILE, 2 * LANES), 0)
    across = lax.broadcasted_iota(jnp.int32, (TILE, 2 * LANES), 1)
    for member in range(rep_count):
        column = jnp.sum(jnp.where(across == tall + member * TILE, wide, 0.0), axis=1, keepdims=True)
        table_ref[member, :TILE] = jnp.broadcast_to(column, (TILE, LANES))
        table_ref[member, TILE:] = jnp.zeros((rows - TILE, LANES), jnp.float32)

    lane = lax.broadcasted_iota(jnp.int32, (rows, LANES), 1)
    spare = LANES - 8
    for steps, out_ref in zip(rounds(groups), out_refs):
        group = partner_of(my_grp, step_of(steps, my_rep), groups)
        tile = group * rep_count + my_rep
        chosen = [tile]
        member, place_of = jnp.int32(0), jnp.int32(-1)
        for slot in range(listed):
            other = pairs_ref[slot, tile]
            chosen.append(jnp.maximum(other, 0))
            inside = (other >= 0) & (lax.div(other, rep_count) == my_grp)
            member = jnp.where(inside, lax.rem(other, rep_count), member)
            place_of = jnp.where(inside, slot + 1, place_of)
        own_at = jnp.where(group == my_grp, spare, -1)
        theirs = table_ref[member]
        mine = table_ref[my_rep]
        for block in range(packed // LANES):
            total = jnp.zeros((rows, LANES), jnp.float32)
            for place in range(PER_BLOCK):
                index = block * PER_BLOCK + place
                if index > listed:
                    continue
                start = chosen[index] * TILE
                source = lax.div(start, LANES)
                offset = lax.rem(start, LANES)
                both = jnp.where(lane >= offset, blocks_ref[source], blocks_ref[source + 1])
                shift = lax.rem(place * TILE + LANES - offset, LANES)
                moved = pltpu.roll(both, shift, 1)
                here = (lane >= place * TILE) & (lane < (place + 1) * TILE)
                total = jnp.where(here, moved, total)
            first = block * PER_BLOCK
            here = (place_of >= first) & (place_of < first + PER_BLOCK)
            marked = jnp.where(here, spare + place_of - first, -1)
            total = jnp.where(lane == marked, theirs, total)
            if block == 0:
                total = jnp.where(lane == own_at, mine, total)
            out_ref[:, block * LANES : (block + 1) * LANES] = total.astype(jnp.bfloat16)
    copies = [
        pltpu.make_async_copy(stage_ref.at[index], out_hbm, sent.at[index])
        for index, out_hbm in enumerate(outs_hbm)
    ]
    for copy in copies:
        copy.start()
    for copy in copies:
        copy.wait()


def pack(strain, fir_taps, half_widths, pairs, groups, rep_count):
    channels, filled = strain.shape
    rows = max(filled, -(-TILE // 16) * 16)
    tiles, listed = pairs.shape
    members = half_widths.shape[0]
    packed = -(-(listed + 1) // PER_BLOCK) * LANES
    hbm = pl.BlockSpec(memory_space=pltpu.HBM)
    vmem = pl.BlockSpec(memory_space=pltpu.VMEM)
    return pl.pallas_call(
        functools.partial(pack_kernel, rep_count),
        out_shape=[pltpu.HBM((rows, packed), jnp.bfloat16)] * groups
        + [jax.ShapeDtypeStruct((1, fir_taps.shape[0]), jnp.float32)],
        in_specs=[hbm] * 4,
        out_specs=[hbm] * groups + [vmem],
        scratch_shapes=[
            pltpu.VMEM((groups, rows, packed), jnp.bfloat16),
            pltpu.SemaphoreType.DMA((groups,)),
            pltpu.SMEM((listed, tiles), jnp.int32),
            pltpu.VMEM((filled, channels), jnp.bfloat16),
            pltpu.VMEM((1, members), jnp.int32),
            pltpu.SemaphoreType.DMA((4,)),
            pltpu.VMEM((channels // LANES + 1, rows, LANES), jnp.float32),
            pltpu.VMEM((rep_count, rows, LANES), jnp.float32),
        ],
        compiler_params=pltpu.CompilerParams(vmem_limit_bytes=48 * 2**20),
        name="pack",
    )(*[
        pltpu.with_memory_space_constraint(array, pltpu.HBM)
        for array in (pairs.T, strain.T, half_widths[None, :], fir_taps[None, :])
    ])


def split(values):
    high = values.astype(jnp.bfloat16)
    low = (values - high.astype(jnp.float32)).astype(jnp.bfloat16)
    return high, low


def dot(left, right):
    return jnp.dot(left, right, preferred_element_type=jnp.float32)


def condition(period, raw_ref, taps_ref, white_ref):
    groups, rows, packed = raw_ref.shape
    listed = white_ref.shape[0] // TILE - 1
    blocks = packed // LANES
    raw = raw_ref[:, :period, :].astype(jnp.float32).reshape(groups * period, packed)
    samples = jnp.transpose(raw).astype(jnp.bfloat16)
    columns = []
    for block in range(blocks):
        piece = raw_ref[:, :TILE, block * LANES : (block + 1) * LANES].astype(jnp.float32)
        columns.append(jnp.sum(piece, axis=0))

    count = taps_ref.shape[1]
    taps = jnp.concatenate([taps_ref[...], jnp.zeros((1, 2 * LANES - count), jnp.float32)], axis=1)
    bands = pltpu.roll(jnp.broadcast_to(taps, (LANES, 2 * LANES)), 0, 1, stride=1, stride_axis=0)
    parts = []
    empty = jnp.zeros((LANES, LANES), jnp.bfloat16)
    for piece in split(bands):
        near, far = piece[:, :LANES], piece[:, LANES:]
        first = jnp.concatenate([piece, jnp.concatenate([empty, near], axis=1)], axis=0)
        second = jnp.concatenate([far, near], axis=0)
        parts.append((dot(samples[:, : 2 * LANES], first), dot(samples[:, LANES:], second)))
    filtered = jnp.concatenate([parts[0][0] + parts[1][0], parts[0][1] + parts[1][1]], axis=1)

    size = jnp.abs(filtered)
    before = lax.broadcasted_iota(jnp.int32, (2 * LANES, 2 * LANES), 0) <= lax.broadcasted_iota(
        jnp.int32, (2 * LANES, 2 * LANES), 1
    )
    upper = jnp.where(before, 1.0, 0.0).astype(jnp.bfloat16)
    ones = jnp.ones((2 * LANES, LANES), jnp.bfloat16)
    sums = []
    for piece in split(size):
        head, tail = piece[:, : 2 * LANES], piece[:, 2 * LANES :]
        sums.append((dot(head, upper), dot(head, ones), dot(tail, upper[:LANES, :LANES])))
    high, low = sums
    head = high[0] + low[0]
    tail = (high[1] + low[1]) + (high[2] + low[2])
    prefix = [head[:, :LANES], head[:, LANES:], tail]

    lane = lax.broadcasted_iota(jnp.int32, (TILE, LANES), 1)
    for slot in range(listed + 1):
        base = slot // PER_BLOCK * LANES + slot % PER_BLOCK * TILE
        at = slice(base, base + TILE)
        from_lane = LANES - 8 + slot % PER_BLOCK
        column = columns[slot // PER_BLOCK][:, from_lane : from_lane + 1]
        width = jnp.broadcast_to(column, (TILE, LANES))
        whole = width.astype(jnp.int32)
        above = lane + whole
        below = lane - whole - 1
        above_at = above & (LANES - 1)
        below_at = below & (LANES - 1)
        above_by = above >> 7
        below_by = below >> 7
        up = [jnp.take_along_axis(prefix[b][at], above_at, axis=1) for b in range(3)]
        down = [jnp.take_along_axis(prefix[b][at], below_at, axis=1) for b in range(2)]
        full = jnp.broadcast_to(prefix[2][at][:, LANES - 1 :], (TILE, LANES))
        ends = up + [full, full]
        starts = [jnp.zeros((TILE, LANES), jnp.float32)] * 2 + down
        down_last = jnp.take_along_axis(prefix[2][at], below_at, axis=1)
        starts.append(down_last)
        scale = 1.0 / (2.0 * width + 1.0)
        high_0, high_1 = above_by == 0, above_by == 1
        low_0, low_1 = below_by == 0, below_by == -1
        for block in range(3 if slot else 1):
            top = jnp.where(high_0, ends[block], jnp.where(high_1, ends[block + 1], ends[block + 2]))
            low_end = jnp.where(
                low_0, starts[block + 2], jnp.where(low_1, starts[block + 1], starts[block])
            )
            level = (top - low_end) * scale
            value = filtered[at, block * LANES : (block + 1) * LANES] / (level + 1e-05)
            if slot:
                value = jnp.where(width > 0.0, value, 0.0)
            white_ref[slot * TILE : (slot + 1) * TILE, block * LANES : (block + 1) * LANES] = value


def condition_kernel(period, taps_ref, *refs):
    received = refs[:-4]
    partner_ref, reverse_ref, raw_ref, white_ref = refs[-4:]
    groups = len(received)
    my_grp = lax.axis_index("grp")
    my_rep = lax.axis_index("rep")
    for steps, ref in zip(rounds(groups), received):
        raw_ref[partner_of(my_grp, step_of(steps, my_rep), groups)] = ref[...]
    condition(period, raw_ref, taps_ref, white_ref)

    partner = white_ref[TILE:, :].astype(jnp.bfloat16)
    rows = partner.shape[0]
    partner_ref[:rows] = partner[:, : 2 * LANES]
    partner_ref[rows:] = partner[:, LANES:]
    own = white_ref[:TILE, :LANES].astype(jnp.bfloat16)
    row = lax.broadcasted_iota(jnp.int32, (LANES, LANES), 0)
    col = lax.broadcasted_iota(jnp.int32, (LANES, LANES), 1)
    flip = jnp.where(row + col == LANES - 1, 1.0, 0.0).astype(jnp.bfloat16)
    reverse_ref[...] = dot(own, flip)


def conditioned(received, taps, period, listed):
    groups = len(received)
    rows, packed = received[0].shape
    vmem = pl.BlockSpec(memory_space=pltpu.VMEM)
    return pl.pallas_call(
        functools.partial(condition_kernel, period),
        out_shape=[
            jax.ShapeDtypeStruct((2 * listed * TILE, 2 * LANES), jnp.bfloat16),
            jax.ShapeDtypeStruct((TILE, LANES), jnp.float32),
        ],
        in_specs=[vmem] * (groups + 1),
        out_specs=[vmem, vmem],
        scratch_shapes=[
            pltpu.VMEM((groups, rows, packed), jnp.bfloat16),
            pltpu.VMEM(((listed + 1) * TILE, groups * period), jnp.float32),
        ],
        compiler_params=pltpu.CompilerParams(vmem_limit_bytes=32 * 2**20),
        name="condition",
    )(taps, *received)


def correlate_kernel(
    partner_ref, reverse_ref, out_hbm, low_even, high_even, low_odd, high_odd, packed_ref, semaphores
):
    listed = out_hbm.shape[1]
    rows = listed * TILE
    normalizer = 1.0 / math.sqrt(LANES)
    keep = lax.broadcasted_iota(jnp.int32, (LANES, LANES), 1) <= lax.broadcasted_iota(
        jnp.int32, (LANES, LANES), 0
    )
    even, odd = (low_even, high_even), (low_odd, high_odd)
    count = TILE // 8
    parts = 4
    share = listed // parts

    def band(channel):
        line = jnp.broadcast_to(reverse_ref[pl.ds(channel, 1), :], (LANES, LANES))
        turned = pltpu.roll(line, 1, 1, stride=1, stride_axis=0)
        first = jnp.where(keep, turned, 0.0).astype(jnp.bfloat16)
        second = jnp.where(keep, 0.0, turned).astype(jnp.bfloat16)
        return jnp.concatenate([first, second], axis=0)

    def outgoing(group, part):
        tiles = pl.ds(part * share, share)
        return pltpu.make_async_copy(
            packed_ref.at[group, tiles],
            out_hbm.at[0, tiles, :, pl.ds(group * 8, 8), :],
            semaphores.at[group, part],
        )

    def multiply(group, part, held):
        channel = group * 8 + 2 * part
        weights = jnp.concatenate([band(channel), band(channel + 1)], axis=1)
        product = dot(partner_ref[...], weights) * normalizer
        for half, ref in enumerate(held):
            for side in range(2):
                ref[pl.ds(2 * part + side, rows, stride=STRIDE), :] = product[
                    half * rows : (half + 1) * rows, side * LANES : (side + 1) * LANES
                ]

    def convert(group, part, held):
        for tile in range(part * share, (part + 1) * share):
            for line in range(TILE):
                at = pl.ds((tile * TILE + line) * STRIDE, 8)
                both = jnp.concatenate([ref[at, :] for ref in held], axis=1)
                packed_ref[group, tile, line] = both.astype(jnp.bfloat16)

    def together(group, held, before):
        for part in range(parts):
            multiply(group, part, held)
            convert(group - 1, part, before)
        for part in range(parts):
            outgoing(group - 1, part).start()

    for part in range(parts):
        multiply(0, part, even)

    def two_groups(index, carry):
        together(2 * index + 1, odd, even)
        together(2 * index + 2, even, odd)
        return carry

    lax.fori_loop(0, count // 2, two_groups, 0)
    for part in range(parts):
        convert(count - 1, part, even)
        outgoing(count - 1, part).start()
    for group in range(count):
        for part in range(parts):
            outgoing(group, part).wait()


def correlate(partner, reverse):
    rows = partner.shape[0] // 2
    listed = rows // TILE
    vmem = pl.BlockSpec(memory_space=pltpu.VMEM)
    return pl.pallas_call(
        correlate_kernel,
        out_shape=jax.ShapeDtypeStruct((1, listed, TILE, TILE, LAGS), jnp.bfloat16),
        in_specs=[vmem, vmem],
        out_specs=pl.BlockSpec(memory_space=pltpu.HBM),
        scratch_shapes=[pltpu.VMEM((rows * STRIDE, LANES), jnp.float32)] * 4
        + [
            pltpu.VMEM((TILE // 8, listed, TILE, 8, LAGS), jnp.bfloat16),
            pltpu.SemaphoreType.DMA((TILE // 8, 4)),
        ],
        compiler_params=pltpu.CompilerParams(vmem_limit_bytes=40 * 2**20),
        name="correlate",
    )(partner, reverse)


def on_device(strain, fir_taps, half_widths, pairs):
    groups = lax.axis_size("grp")
    rep_count = lax.axis_size("rep")
    *messages, taps = pack(strain, fir_taps, half_widths, pairs, groups, rep_count)
    received = []
    for steps, message in zip(rounds(groups), messages):
        if steps == (0, 0):
            received.append(message)
            continue
        route = [
            (
                group * rep_count + member,
                partner_of(group, steps[member % 2], groups) * rep_count + member,
            )
            for group in range(groups)
            for member in range(rep_count)
        ]
        received.append(lax.ppermute(message, ("grp", "rep"), route))
    partner, reverse = conditioned(received, taps, strain.shape[1], pairs.shape[1])
    return correlate(partner, reverse)


def solution(mesh):
    placed = (P(None, "grp"), P(), P("grp"), P())
    return jax.shard_map(
        on_device,
        mesh=mesh,
        in_specs=placed,
        out_specs=P(("grp", "rep"), None, None, None, None),
        check_vma=False,
    )
```

```python
import functools
import math

import jax
import jax.numpy as jnp
from jax import lax
from jax.experimental import pallas as pl
from jax.experimental.pallas import tpu as pltpu
from jax.sharding import PartitionSpec as P

TILE = 40
LAGS = 256
LANES = 128
STRIDE = 9
PER_BLOCK = LANES // TILE


def fetch(pairs, semaphores):
    copies = [
        pltpu.make_async_copy(source, target, semaphores.at[index])
        for index, (source, target) in enumerate(pairs)
    ]
    for copy in copies:
        copy.start()
    for copy in copies:
        copy.wait()


def gather_tiles(groups, rep_count, source, pairs_ref, strain_ref, widths_ref, blocks_ref, table_ref, write):
    rows = blocks_ref.shape[1]
    filled, channels = strain_ref.shape
    listed = pairs_ref.shape[0]
    packed = -(-(listed + 1) // PER_BLOCK) * LANES
    members = widths_ref.shape[1]
    my_rep = lax.axis_index("rep")
    my_grp = lax.axis_index("grp")

    count = channels // LANES
    for block in range(count):
        values = strain_ref[:, block * LANES : (block + 1) * LANES].astype(jnp.float32)
        if rows > filled:
            values = jnp.concatenate([values, jnp.zeros((rows - filled, LANES), jnp.float32)], axis=0)
        blocks_ref[block] = values
    blocks_ref[count] = jnp.zeros((rows, LANES), jnp.float32)

    wide = jnp.concatenate(
        [widths_ref[...].astype(jnp.float32), jnp.zeros((1, 2 * LANES - members), jnp.float32)],
        axis=1,
    )
    wide = jnp.broadcast_to(wide, (TILE, 2 * LANES))
    tall = lax.broadcasted_iota(jnp.int32, (TILE, 2 * LANES), 0)
    across = lax.broadcasted_iota(jnp.int32, (TILE, 2 * LANES), 1)
    for member in range(rep_count):
        column = jnp.sum(jnp.where(across == tall + member * TILE, wide, 0.0), axis=1, keepdims=True)
        table_ref[member, :TILE] = jnp.broadcast_to(column, (TILE, LANES))
        table_ref[member, TILE:] = jnp.zeros((rows - TILE, LANES), jnp.float32)

    lane = lax.broadcasted_iota(jnp.int32, (rows, LANES), 1)
    spare = LANES - 8
    for step in rounds(groups):
        group = lax.rem(my_grp + 2 * step, groups)
        tile = group * rep_count + my_rep
        chosen = [tile]
        member, place_of = jnp.int32(0), jnp.int32(-1)
        for slot in range(listed):
            other = pairs_ref[slot, tile]
            chosen.append(jnp.maximum(other, 0))
            inside = (other >= 0) & (lax.div(other, rep_count) == source)
            member = jnp.where(inside, lax.rem(other, rep_count), member)
            place_of = jnp.where(inside, slot + 1, place_of)
        own_at = jnp.where(group == source, spare, -1)
        theirs = table_ref[member]
        mine = table_ref[my_rep]
        for block in range(packed // LANES):
            total = jnp.zeros((rows, LANES), jnp.float32)
            for place in range(PER_BLOCK):
                index = block * PER_BLOCK + place
                if index > listed:
                    continue
                start = chosen[index] * TILE
                at = lax.div(start, LANES)
                offset = lax.rem(start, LANES)
                both = jnp.where(lane >= offset, blocks_ref[at], blocks_ref[at + 1])
                shift = lax.rem(place * TILE + LANES - offset, LANES)
                moved = pltpu.roll(both, shift, 1)
                here = (lane >= place * TILE) & (lane < (place + 1) * TILE)
                total = jnp.where(here, moved, total)
            first = block * PER_BLOCK
            here = (place_of >= first) & (place_of < first + PER_BLOCK)
            marked = jnp.where(here, spare + place_of - first, -1)
            total = jnp.where(lane == marked, theirs, total)
            if block == 0:
                total = jnp.where(lane == own_at, mine, total)
            write(step, slice(block * LANES, (block + 1) * LANES), total.astype(jnp.bfloat16))


def rounds(groups):
    return list(range(1, groups // 2)) + [0]


def fetch(pairs, semaphores):
    copies = [
        pltpu.make_async_copy(source, target, semaphores.at[index])
        for index, (source, target) in enumerate(pairs)
    ]
    for copy in copies:
        copy.start()
    for copy in copies:
        copy.wait()


def pack_own_kernel(
    groups, rep_count, pairs_hbm, strain_hbm, widths_hbm, taps_hbm, out_ref, list_ref, taps_ref,
    pairs_ref, strain_ref, widths_ref, semaphores, blocks_ref, table_ref,
):
    fetch(
        [
            (strain_hbm, strain_ref),
            (pairs_hbm, pairs_ref),
            (widths_hbm, widths_ref),
            (pairs_hbm, list_ref),
            (taps_hbm, taps_ref),
        ],
        semaphores,
    )

    def write(step, at, value):
        out_ref[step, :, at] = value

    gather_tiles(
        groups, rep_count, lax.axis_index("grp"), pairs_ref, strain_ref, widths_ref, blocks_ref, table_ref, write
    )


def pack_both_kernel(groups, rep_count, list_ref, widths_ref, strain_ref, own_ref, *refs):
    out_refs = refs[:-4]
    pairs_ref, semaphores, blocks_ref, table_ref = refs[-4:]
    fetch([(list_ref, pairs_ref)], semaphores)
    my_grp = lax.axis_index("grp")
    side = lax.rem(my_grp, 2)
    by_step = dict(zip(rounds(groups), out_refs))
    for step, out_ref in by_step.items():
        out_ref[side] = own_ref[step]

    def write(step, at, value):
        by_step[step][1 - side, :, at] = value

    gather_tiles(groups, rep_count, my_grp ^ 1, pairs_ref, strain_ref, widths_ref, blocks_ref, table_ref, write)


def pack(strain, other_strain, fir_taps, half_widths, other_widths, pairs, groups, rep_count):
    channels, filled = strain.shape
    rows = max(filled, -(-TILE // 16) * 16)
    tiles, listed = pairs.shape
    members = half_widths.shape[0]
    packed = -(-(listed + 1) // PER_BLOCK) * LANES
    halves = groups // 2
    hbm = pl.BlockSpec(memory_space=pltpu.HBM)
    vmem = pl.BlockSpec(memory_space=pltpu.VMEM)
    work = [
        pltpu.VMEM((channels // LANES + 1, rows, LANES), jnp.float32),
        pltpu.VMEM((rep_count, rows, LANES), jnp.float32),
    ]
    params = pltpu.CompilerParams(vmem_limit_bytes=32 * 2**20)
    own, chosen, taps = pl.pallas_call(
        functools.partial(pack_own_kernel, groups, rep_count),
        out_shape=[
            jax.ShapeDtypeStruct((halves, rows, packed), jnp.bfloat16),
            jax.ShapeDtypeStruct((listed, tiles), jnp.int32),
            jax.ShapeDtypeStruct((1, fir_taps.shape[0]), jnp.float32),
        ],
        in_specs=[hbm] * 4,
        out_specs=[vmem] * 3,
        scratch_shapes=[
            pltpu.SMEM((listed, tiles), jnp.int32),
            pltpu.VMEM((filled, channels), jnp.bfloat16),
            pltpu.VMEM((1, members), jnp.int32),
            pltpu.SemaphoreType.DMA((5,)),
        ]
        + work,
        compiler_params=params,
        name="pack_own",
    )(*[
        pltpu.with_memory_space_constraint(array, pltpu.HBM)
        for array in (pairs.T, strain.T, half_widths[None, :], fir_taps[None, :])
    ])
    messages = pl.pallas_call(
        functools.partial(pack_both_kernel, groups, rep_count),
        out_shape=[jax.ShapeDtypeStruct((2, rows, packed), jnp.bfloat16)] * halves,
        in_specs=[vmem] * 4,
        out_specs=[vmem] * halves,
        scratch_shapes=[pltpu.SMEM((listed, tiles), jnp.int32), pltpu.SemaphoreType.DMA((1,))] + work,
        compiler_params=params,
        name="pack_both",
    )(chosen, other_widths[None, :], other_strain, own)
    return messages, taps


def split(values):
    high = values.astype(jnp.bfloat16)
    low = (values - high.astype(jnp.float32)).astype(jnp.bfloat16)
    return high, low


def dot(left, right):
    return jnp.dot(left, right, preferred_element_type=jnp.float32)


def condition(period, raw_ref, taps_ref, white_ref):
    halves, _, rows, packed = raw_ref.shape
    groups = 2 * halves
    listed = white_ref.shape[0] // TILE - 1
    blocks = packed // LANES
    raw = raw_ref[:, :, :period, :].astype(jnp.float32).reshape(groups * period, packed)
    samples = jnp.transpose(raw).astype(jnp.bfloat16)
    columns = []
    for block in range(blocks):
        piece = raw_ref[:, :, :TILE, block * LANES : (block + 1) * LANES].astype(jnp.float32)
        columns.append(jnp.sum(piece.reshape(groups, TILE, LANES), axis=0))

    count = taps_ref.shape[1]
    taps = jnp.concatenate([taps_ref[...], jnp.zeros((1, 2 * LANES - count), jnp.float32)], axis=1)
    bands = pltpu.roll(jnp.broadcast_to(taps, (LANES, 2 * LANES)), 0, 1, stride=1, stride_axis=0)
    parts = []
    empty = jnp.zeros((LANES, LANES), jnp.bfloat16)
    for piece in split(bands):
        near, far = piece[:, :LANES], piece[:, LANES:]
        first = jnp.concatenate([piece, jnp.concatenate([empty, near], axis=1)], axis=0)
        second = jnp.concatenate([far, near], axis=0)
        parts.append((dot(samples[:, : 2 * LANES], first), dot(samples[:, LANES:], second)))
    filtered = jnp.concatenate([parts[0][0] + parts[1][0], parts[0][1] + parts[1][1]], axis=1)

    size = jnp.abs(filtered)
    before = lax.broadcasted_iota(jnp.int32, (2 * LANES, 2 * LANES), 0) <= lax.broadcasted_iota(
        jnp.int32, (2 * LANES, 2 * LANES), 1
    )
    upper = jnp.where(before, 1.0, 0.0).astype(jnp.bfloat16)
    ones = jnp.ones((2 * LANES, LANES), jnp.bfloat16)
    sums = []
    for piece in split(size):
        head, tail = piece[:, : 2 * LANES], piece[:, 2 * LANES :]
        sums.append((dot(head, upper), dot(head, ones), dot(tail, upper[:LANES, :LANES])))
    high, low = sums
    head = high[0] + low[0]
    tail = (high[1] + low[1]) + (high[2] + low[2])
    prefix = [head[:, :LANES], head[:, LANES:], tail]

    lane = lax.broadcasted_iota(jnp.int32, (TILE, LANES), 1)
    for slot in range(listed + 1):
        base = slot // PER_BLOCK * LANES + slot % PER_BLOCK * TILE
        at = slice(base, base + TILE)
        from_lane = LANES - 8 + slot % PER_BLOCK
        column = columns[slot // PER_BLOCK][:, from_lane : from_lane + 1]
        width = jnp.broadcast_to(column, (TILE, LANES))
        whole = width.astype(jnp.int32)
        above = lane + whole
        below = lane - whole - 1
        above_at = above & (LANES - 1)
        below_at = below & (LANES - 1)
        above_by = above >> 7
        below_by = below >> 7
        up = [jnp.take_along_axis(prefix[b][at], above_at, axis=1) for b in range(3)]
        down = [jnp.take_along_axis(prefix[b][at], below_at, axis=1) for b in range(2)]
        full = jnp.broadcast_to(prefix[2][at][:, LANES - 1 :], (TILE, LANES))
        ends = up + [full, full]
        starts = [jnp.zeros((TILE, LANES), jnp.float32)] * 2 + down
        down_last = jnp.take_along_axis(prefix[2][at], below_at, axis=1)
        starts.append(down_last)
        scale = 1.0 / (2.0 * width + 1.0)
        high_0, high_1 = above_by == 0, above_by == 1
        low_0, low_1 = below_by == 0, below_by == -1
        for block in range(3 if slot else 1):
            top = jnp.where(high_0, ends[block], jnp.where(high_1, ends[block + 1], ends[block + 2]))
            low_end = jnp.where(
                low_0, starts[block + 2], jnp.where(low_1, starts[block + 1], starts[block])
            )
            level = (top - low_end) * scale
            value = filtered[at, block * LANES : (block + 1) * LANES] / (level + 1e-05)
            if slot:
                value = jnp.where(width > 0.0, value, 0.0)
            white_ref[slot * TILE : (slot + 1) * TILE, block * LANES : (block + 1) * LANES] = value


def condition_kernel(period, taps_ref, *refs):
    received = refs[:-4]
    partner_ref, reverse_ref, raw_ref, white_ref = refs[-4:]
    halves = len(received)
    my_half = lax.div(lax.axis_index("grp"), 2)
    for step, ref in zip(rounds(2 * halves), received):
        raw_ref[lax.rem(my_half + halves - step, halves)] = ref[...]
    condition(period, raw_ref, taps_ref, white_ref)

    partner = white_ref[TILE:, :].astype(jnp.bfloat16)
    rows = partner.shape[0]
    partner_ref[:rows] = partner[:, : 2 * LANES]
    partner_ref[rows:] = partner[:, LANES:]
    own = white_ref[:TILE, :LANES].astype(jnp.bfloat16)
    row = lax.broadcasted_iota(jnp.int32, (LANES, LANES), 0)
    col = lax.broadcasted_iota(jnp.int32, (LANES, LANES), 1)
    flip = jnp.where(row + col == LANES - 1, 1.0, 0.0).astype(jnp.bfloat16)
    reverse_ref[...] = dot(own, flip)


def conditioned(received, taps, period, listed):
    halves = len(received)
    _, rows, packed = received[0].shape
    vmem = pl.BlockSpec(memory_space=pltpu.VMEM)
    return pl.pallas_call(
        functools.partial(condition_kernel, period),
        out_shape=[
            jax.ShapeDtypeStruct((2 * listed * TILE, 2 * LANES), jnp.bfloat16),
            jax.ShapeDtypeStruct((TILE, LANES), jnp.float32),
        ],
        in_specs=[vmem] * (halves + 1),
        out_specs=[vmem, vmem],
        scratch_shapes=[
            pltpu.VMEM((halves, 2, rows, packed), jnp.bfloat16),
            pltpu.VMEM(((listed + 1) * TILE, 2 * halves * period), jnp.float32),
        ],
        compiler_params=pltpu.CompilerParams(vmem_limit_bytes=32 * 2**20),
        name="condition",
    )(taps, *received)


def correlate_kernel(
    partner_ref, reverse_ref, out_hbm, low_even, high_even, low_odd, high_odd, packed_ref, semaphores
):
    listed = out_hbm.shape[1]
    rows = listed * TILE
    normalizer = 1.0 / math.sqrt(LANES)
    keep = lax.broadcasted_iota(jnp.int32, (LANES, LANES), 1) <= lax.broadcasted_iota(
        jnp.int32, (LANES, LANES), 0
    )
    even, odd = (low_even, high_even), (low_odd, high_odd)
    count = TILE // 8
    parts = 4
    share = listed // parts

    def band(channel):
        line = jnp.broadcast_to(reverse_ref[pl.ds(channel, 1), :], (LANES, LANES))
        turned = pltpu.roll(line, 1, 1, stride=1, stride_axis=0)
        first = jnp.where(keep, turned, 0.0).astype(jnp.bfloat16)
        second = jnp.where(keep, 0.0, turned).astype(jnp.bfloat16)
        return jnp.concatenate([first, second], axis=0)

    def outgoing(group, part):
        tiles = pl.ds(part * share, share)
        return pltpu.make_async_copy(
            packed_ref.at[group, tiles],
            out_hbm.at[0, tiles, :, pl.ds(group * 8, 8), :],
            semaphores.at[group, part],
        )

    def multiply(group, part, held):
        channel = group * 8 + 2 * part
        weights = jnp.concatenate([band(channel), band(channel + 1)], axis=1)
        product = dot(partner_ref[...], weights) * normalizer
        for half, ref in enumerate(held):
            for side in range(2):
                ref[pl.ds(2 * part + side, rows, stride=STRIDE), :] = product[
                    half * rows : (half + 1) * rows, side * LANES : (side + 1) * LANES
                ]

    def convert(group, part, held):
        for tile in range(part * share, (part + 1) * share):
            for line in range(TILE):
                at = pl.ds((tile * TILE + line) * STRIDE, 8)
                both = jnp.concatenate([ref[at, :] for ref in held], axis=1)
                packed_ref[group, tile, line] = both.astype(jnp.bfloat16)

    def together(group, held, before):
        for part in range(parts):
            multiply(group, part, held)
            convert(group - 1, part, before)
        for part in range(parts):
            outgoing(group - 1, part).start()

    for part in range(parts):
        multiply(0, part, even)

    def two_groups(index, carry):
        together(2 * index + 1, odd, even)
        together(2 * index + 2, even, odd)
        return carry

    lax.fori_loop(0, count // 2, two_groups, 0)
    for part in range(parts):
        convert(count - 1, part, even)
        outgoing(count - 1, part).start()
    for group in range(count):
        for part in range(parts):
            outgoing(group, part).wait()


def correlate(partner, reverse):
    rows = partner.shape[0] // 2
    listed = rows // TILE
    vmem = pl.BlockSpec(memory_space=pltpu.VMEM)
    return pl.pallas_call(
        correlate_kernel,
        out_shape=jax.ShapeDtypeStruct((1, listed, TILE, TILE, LAGS), jnp.bfloat16),
        in_specs=[vmem, vmem],
        out_specs=pl.BlockSpec(memory_space=pltpu.HBM),
        scratch_shapes=[pltpu.VMEM((rows * STRIDE, LANES), jnp.float32)] * 4
        + [
            pltpu.VMEM((TILE // 8, listed, TILE, 8, LAGS), jnp.bfloat16),
            pltpu.SemaphoreType.DMA((TILE // 8, 4)),
        ],
        compiler_params=pltpu.CompilerParams(vmem_limit_bytes=40 * 2**20),
        name="correlate",
    )(partner, reverse)


def on_device(strain, fir_taps, half_widths, pairs):
    groups = lax.axis_size("grp")
    rep_count = lax.axis_size("rep")
    neighbours = [(group, group ^ 1) for group in range(groups)]
    other_widths = lax.ppermute(half_widths, "grp", neighbours)
    other_strain = lax.ppermute(strain.T, "grp", neighbours)
    messages, taps = pack(
        strain, other_strain, fir_taps, half_widths, other_widths, pairs, groups, rep_count
    )
    received = []
    for step, message in zip(rounds(groups), messages):
        if step:
            route = [(group, (group + 2 * step) % groups) for group in range(groups)]
            message = lax.ppermute(message, "grp", route)
        received.append(message)
    partner, reverse = conditioned(received, taps, strain.shape[1], pairs.shape[1])
    return correlate(partner, reverse)


def solution(mesh):
    placed = (P(None, "grp"), P(), P("grp"), P())
    return jax.shard_map(
        on_device,
        mesh=mesh,
        in_specs=placed,
        out_specs=P(("grp", "rep"), None, None, None, None),
        check_vma=False,
    )
```

```python
import functools
import math

import jax
import jax.numpy as jnp
from jax import lax
from jax.experimental import pallas as pl
from jax.experimental.pallas import tpu as pltpu
from jax.sharding import PartitionSpec as P

TILE = 40
LAGS = 256
LANES = 128
STRIDE = 9
PER_BLOCK = LANES // TILE


def fetch(pairs, semaphores):
    copies = [
        pltpu.make_async_copy(source, target, semaphores.at[index])
        for index, (source, target) in enumerate(pairs)
    ]
    for copy in copies:
        copy.start()
    for copy in copies:
        copy.wait()


ROUTES = (
    (2, 3, 5, 4, 7, 6, 1, 0),
    (1, 0, 3, 2, 5, 4, 7, 6),
    (3, 2, 4, 5, 6, 7, 0, 1),
    (4, 5, 7, 6, 1, 0, 2, 3),
    (6, 7, 1, 0, 2, 3, 4, 5),
    (5, 4, 6, 7, 0, 1, 3, 2),
    (7, 6, 0, 1, 3, 2, 5, 4),
)


def routes(groups):
    if groups == len(ROUTES[0]):
        return list(ROUTES) + [tuple(range(groups))]
    return [tuple(group ^ step for group in range(groups)) for step in reversed(range(groups))]


def inverse(route):
    return tuple(route.index(group) for group in range(len(route)))


def pick(route, group):
    if len(route) > 8:
        return group ^ route[0]
    code = sum(target << (3 * index) for index, target in enumerate(route))
    return (jnp.int32(code) >> (3 * group)) & 7


def pack_kernel(rep_count, pairs_hbm, strain_hbm, widths_hbm, taps_hbm, *refs):
    out_refs = refs[:-7]
    taps_ref = refs[-7]
    pairs_ref, strain_ref, widths_ref, semaphores, blocks_ref, table_ref = refs[-6:]
    groups = len(out_refs)
    rows, packed = out_refs[0].shape
    listed = pairs_ref.shape[0]
    channels = strain_ref.shape[1]
    members = widths_ref.shape[1]
    fetch(
        [
            (strain_hbm, strain_ref),
            (pairs_hbm, pairs_ref),
            (widths_hbm, widths_ref),
            (taps_hbm, taps_ref),
        ],
        semaphores,
    )
    my_rep = lax.axis_index("rep")
    my_grp = lax.axis_index("grp")

    count = channels // LANES
    filled = strain_ref.shape[0]
    for block in range(count):
        values = strain_ref[:, block * LANES : (block + 1) * LANES].astype(jnp.float32)
        if rows > filled:
            values = jnp.concatenate([values, jnp.zeros((rows - filled, LANES), jnp.float32)], axis=0)
        blocks_ref[block] = values
    blocks_ref[count] = jnp.zeros((rows, LANES), jnp.float32)

    wide = jnp.concatenate(
        [widths_ref[...].astype(jnp.float32), jnp.zeros((1, 2 * LANES - members), jnp.float32)],
        axis=1,
    )
    wide = jnp.broadcast_to(wide, (TILE, 2 * LANES))
    tall = lax.broadcasted_iota(jnp.int32, (TILE, 2 * LANES), 0)
    across = lax.broadcasted_iota(jnp.int32, (TILE, 2 * LANES), 1)
    for member in range(rep_count):
        column = jnp.sum(jnp.where(across == tall + member * TILE, wide, 0.0), axis=1, keepdims=True)
        table_ref[member, :TILE] = jnp.broadcast_to(column, (TILE, LANES))
        table_ref[member, TILE:] = jnp.zeros((rows - TILE, LANES), jnp.float32)

    lane = lax.broadcasted_iota(jnp.int32, (rows, LANES), 1)
    spare = LANES - 8
    for route, out_ref in zip(routes(groups), out_refs):
        group = pick(route, my_grp)
        tile = group * rep_count + my_rep
        chosen = [tile]
        member, place_of = jnp.int32(0), jnp.int32(-1)
        for slot in range(listed):
            other = pairs_ref[slot, tile]
            chosen.append(jnp.maximum(other, 0))
            among = other - my_grp * rep_count
            inside = (among >= 0) & (among < rep_count)
            member = jnp.where(inside, among, member)
            place_of = jnp.where(inside, slot + 1, place_of)
        own_at = jnp.where(group == my_grp, spare, -1)
        theirs = table_ref[member]
        mine = table_ref[my_rep]
        for block in range(packed // LANES):
            total = jnp.zeros((rows, LANES), jnp.float32)
            for place in range(PER_BLOCK):
                index = block * PER_BLOCK + place
                if index > listed:
                    continue
                start = chosen[index] * TILE
                source = start >> 7
                offset = start & (LANES - 1)
                both = jnp.where(lane >= offset, blocks_ref[source], blocks_ref[source + 1])
                shift = (place * TILE - offset) & (LANES - 1)
                moved = pltpu.roll(both, shift, 1)
                here = (lane >= place * TILE) & (lane < (place + 1) * TILE)
                total = jnp.where(here, moved, total)
            first = block * PER_BLOCK
            here = (place_of >= first) & (place_of < first + PER_BLOCK)
            marked = jnp.where(here, spare + place_of - first, -1)
            total = jnp.where(lane == marked, theirs, total)
            if block == 0:
                total = jnp.where(lane == own_at, mine, total)
            out_ref[:, block * LANES : (block + 1) * LANES] = total.astype(jnp.bfloat16)


def pack(strain, fir_taps, half_widths, pairs, groups, rep_count):
    channels, filled = strain.shape
    rows = max(filled, -(-TILE // 16) * 16)
    tiles, listed = pairs.shape
    members = half_widths.shape[0]
    packed = -(-(listed + 1) // PER_BLOCK) * LANES
    hbm = pl.BlockSpec(memory_space=pltpu.HBM)
    vmem = pl.BlockSpec(memory_space=pltpu.VMEM)
    return pl.pallas_call(
        functools.partial(pack_kernel, rep_count),
        out_shape=[jax.ShapeDtypeStruct((rows, packed), jnp.bfloat16)] * groups
        + [jax.ShapeDtypeStruct((1, fir_taps.shape[0]), jnp.float32)],
        in_specs=[hbm] * 4,
        out_specs=[vmem] * (groups + 1),
        scratch_shapes=[
            pltpu.SMEM((listed, tiles), jnp.int32),
            pltpu.VMEM((filled, channels), jnp.bfloat16),
            pltpu.VMEM((1, members), jnp.int32),
            pltpu.SemaphoreType.DMA((4,)),
            pltpu.VMEM((channels // LANES + 1, rows, LANES), jnp.float32),
            pltpu.VMEM((rep_count, rows, LANES), jnp.float32),
        ],
        compiler_params=pltpu.CompilerParams(vmem_limit_bytes=48 * 2**20),
        name="pack",
    )(*[
        pltpu.with_memory_space_constraint(array, pltpu.HBM)
        for array in (pairs.T, strain.T, half_widths[None, :], fir_taps[None, :])
    ])


def split(values):
    high = values.astype(jnp.bfloat16)
    low = (values - high.astype(jnp.float32)).astype(jnp.bfloat16)
    return high, low


def dot(left, right):
    return jnp.dot(left, right, preferred_element_type=jnp.float32)


def condition(period, raw_ref, taps_ref, white_ref):
    groups, rows, packed = raw_ref.shape
    listed = white_ref.shape[0] // TILE - 1
    blocks = packed // LANES
    raw = raw_ref[:, :period, :].astype(jnp.float32).reshape(groups * period, packed)
    samples = jnp.transpose(raw).astype(jnp.bfloat16)
    columns = []
    for block in range(blocks):
        piece = raw_ref[:, :TILE, block * LANES : (block + 1) * LANES].astype(jnp.float32)
        columns.append(jnp.sum(piece, axis=0))

    count = taps_ref.shape[1]
    taps = jnp.concatenate([taps_ref[...], jnp.zeros((1, 2 * LANES - count), jnp.float32)], axis=1)
    bands = pltpu.roll(jnp.broadcast_to(taps, (LANES, 2 * LANES)), 0, 1, stride=1, stride_axis=0)
    parts = []
    empty = jnp.zeros((LANES, LANES), jnp.bfloat16)
    for piece in split(bands):
        near, far = piece[:, :LANES], piece[:, LANES:]
        first = jnp.concatenate([piece, jnp.concatenate([empty, near], axis=1)], axis=0)
        second = jnp.concatenate([far, near], axis=0)
        parts.append((dot(samples[:, : 2 * LANES], first), dot(samples[:, LANES:], second)))
    filtered = jnp.concatenate([parts[0][0] + parts[1][0], parts[0][1] + parts[1][1]], axis=1)

    size = jnp.abs(filtered)
    before = lax.broadcasted_iota(jnp.int32, (2 * LANES, 2 * LANES), 0) <= lax.broadcasted_iota(
        jnp.int32, (2 * LANES, 2 * LANES), 1
    )
    upper = jnp.where(before, 1.0, 0.0).astype(jnp.bfloat16)
    ones = jnp.ones((2 * LANES, LANES), jnp.bfloat16)
    sums = []
    for piece in split(size):
        head, tail = piece[:, : 2 * LANES], piece[:, 2 * LANES :]
        sums.append((dot(head, upper), dot(head, ones), dot(tail, upper[:LANES, :LANES])))
    high, low = sums
    head = high[0] + low[0]
    tail = (high[1] + low[1]) + (high[2] + low[2])
    prefix = [head[:, :LANES], head[:, LANES:], tail]

    lane = lax.broadcasted_iota(jnp.int32, (TILE, LANES), 1)
    for slot in range(listed + 1):
        base = slot // PER_BLOCK * LANES + slot % PER_BLOCK * TILE
        at = slice(base, base + TILE)
        from_lane = LANES - 8 + slot % PER_BLOCK
        column = columns[slot // PER_BLOCK][:, from_lane : from_lane + 1]
        width = jnp.broadcast_to(column, (TILE, LANES))
        whole = width.astype(jnp.int32)
        above = lane + whole
        below = lane - whole - 1
        above_at = above & (LANES - 1)
        below_at = below & (LANES - 1)
        above_by = above >> 7
        below_by = below >> 7
        up = [jnp.take_along_axis(prefix[b][at], above_at, axis=1) for b in range(3)]
        down = [jnp.take_along_axis(prefix[b][at], below_at, axis=1) for b in range(2)]
        full = jnp.broadcast_to(prefix[2][at][:, LANES - 1 :], (TILE, LANES))
        ends = up + [full, full]
        starts = [jnp.zeros((TILE, LANES), jnp.float32)] * 2 + down
        down_last = jnp.take_along_axis(prefix[2][at], below_at, axis=1)
        starts.append(down_last)
        scale = 1.0 / (2.0 * width + 1.0)
        high_0, high_1 = above_by == 0, above_by == 1
        low_0, low_1 = below_by == 0, below_by == -1
        for block in range(3 if slot else 1):
            top = jnp.where(high_0, ends[block], jnp.where(high_1, ends[block + 1], ends[block + 2]))
            low_end = jnp.where(
                low_0, starts[block + 2], jnp.where(low_1, starts[block + 1], starts[block])
            )
            level = (top - low_end) * scale
            value = filtered[at, block * LANES : (block + 1) * LANES] / (level + 1e-05)
            if slot:
                value = jnp.where(width > 0.0, value, 0.0)
            white_ref[slot * TILE : (slot + 1) * TILE, block * LANES : (block + 1) * LANES] = value


def correlate_kernel(period, taps_ref, *refs):
    received = refs[:-11]
    out_hbm, raw_ref, white_ref, partner_ref, reverse_ref = refs[-11:-6]
    low_even, high_even, low_odd, high_odd, packed_ref, semaphores = refs[-6:]
    groups = len(received)
    my_grp = lax.axis_index("grp")
    for route, ref in zip(routes(groups), received):
        raw_ref[pick(inverse(route), my_grp)] = ref[...]
    condition(period, raw_ref, taps_ref, white_ref)

    own = white_ref[:TILE, :LANES].astype(jnp.bfloat16)
    row = lax.broadcasted_iota(jnp.int32, (LANES, LANES), 0)
    col = lax.broadcasted_iota(jnp.int32, (LANES, LANES), 1)
    flip = jnp.where(row + col == LANES - 1, 1.0, 0.0).astype(jnp.bfloat16)
    reverse_ref[...] = dot(own, flip)
    partner = white_ref[TILE:, :].astype(jnp.bfloat16)
    rows = partner.shape[0]
    partner_ref[:rows] = partner[:, : 2 * LANES]
    partner_ref[rows:] = partner[:, LANES:]
    listed = rows // TILE
    normalizer = 1.0 / math.sqrt(LANES)
    keep = col <= row
    even, odd = (low_even, high_even), (low_odd, high_odd)
    count = TILE // 8
    parts = 4
    share = listed // parts

    def band(channel):
        line = jnp.broadcast_to(reverse_ref[pl.ds(channel, 1), :], (LANES, LANES))
        turned = pltpu.roll(line, 1, 1, stride=1, stride_axis=0)
        first = jnp.where(keep, turned, 0.0).astype(jnp.bfloat16)
        second = jnp.where(keep, 0.0, turned).astype(jnp.bfloat16)
        return jnp.concatenate([first, second], axis=0)

    def outgoing(group, part):
        tiles = pl.ds(part * share, share)
        return pltpu.make_async_copy(
            packed_ref.at[group, tiles],
            out_hbm.at[0, tiles, :, pl.ds(group * 8, 8), :],
            semaphores.at[group, part],
        )

    def multiply(group, part, held):
        channel = group * 8 + 2 * part
        weights = jnp.concatenate([band(channel), band(channel + 1)], axis=1)
        product = dot(partner_ref[...], weights) * normalizer
        for half, ref in enumerate(held):
            for side in range(2):
                ref[pl.ds(2 * part + side, rows, stride=STRIDE), :] = product[
                    half * rows : (half + 1) * rows, side * LANES : (side + 1) * LANES
                ]

    def convert(group, part, held):
        for tile in range(part * share, (part + 1) * share):
            for line in range(TILE):
                at = pl.ds((tile * TILE + line) * STRIDE, 8)
                both = jnp.concatenate([ref[at, :] for ref in held], axis=1)
                packed_ref[group, tile, line] = both.astype(jnp.bfloat16)

    def together(group, held, before):
        for part in range(parts):
            multiply(group, part, held)
            convert(group - 1, part, before)
            outgoing(group - 1, part).start()

    for part in range(parts):
        multiply(0, part, even)

    def two_groups(index, carry):
        together(2 * index + 1, odd, even)
        together(2 * index + 2, even, odd)
        return carry

    lax.fori_loop(0, count // 2, two_groups, 0)
    for part in range(parts):
        convert(count - 1, part, even)
        outgoing(count - 1, part).start()
    for group in range(count):
        for part in range(parts):
            outgoing(group, part).wait()


def correlate(received, taps, period, listed):
    groups = len(received)
    rows, packed = received[0].shape
    lines = listed * TILE
    vmem = pl.BlockSpec(memory_space=pltpu.VMEM)
    return pl.pallas_call(
        functools.partial(correlate_kernel, period),
        out_shape=jax.ShapeDtypeStruct((1, listed, TILE, TILE, LAGS), jnp.bfloat16),
        in_specs=[vmem] * (groups + 1),
        out_specs=pl.BlockSpec(memory_space=pltpu.HBM),
        scratch_shapes=[
            pltpu.VMEM((groups, rows, packed), jnp.bfloat16),
            pltpu.VMEM(((listed + 1) * TILE, groups * period), jnp.float32),
            pltpu.VMEM((2 * lines, 2 * LANES), jnp.bfloat16),
            pltpu.VMEM((TILE, LANES), jnp.float32),
        ]
        + [pltpu.VMEM((lines * STRIDE, LANES), jnp.float32)] * 4
        + [
            pltpu.VMEM((TILE // 8, listed, TILE, 8, LAGS), jnp.bfloat16),
            pltpu.SemaphoreType.DMA((TILE // 8, 4)),
        ],
        compiler_params=pltpu.CompilerParams(vmem_limit_bytes=40 * 2**20),
        name="correlate",
    )(taps, *received)


def on_device(strain, fir_taps, half_widths, pairs):
    groups = lax.axis_size("grp")
    rep_count = lax.axis_size("rep")
    *messages, taps = pack(strain, fir_taps, half_widths, pairs, groups, rep_count)
    received = []
    for route, message in zip(routes(groups), messages):
        if route != tuple(range(groups)):
            message = lax.ppermute(message, "grp", list(enumerate(route)))
        received.append(message)
    return correlate(received, taps, strain.shape[1], pairs.shape[1])


def solution(mesh):
    placed = (P(None, "grp"), P(), P("grp"), P())
    return jax.shard_map(
        on_device,
        mesh=mesh,
        in_specs=placed,
        out_specs=P(("grp", "rep"), None, None, None, None),
        check_vma=False,
    )
```

```python
import functools
import math

import jax
import jax.numpy as jnp
from jax import lax
from jax.experimental import pallas as pl
from jax.experimental.pallas import tpu as pltpu
from jax.sharding import PartitionSpec as P

TILE = 40
LAGS = 256
LANES = 128
STRIDE = 9
PER_BLOCK = LANES // TILE


def fetch(pairs, semaphores):
    copies = [
        pltpu.make_async_copy(source, target, semaphores.at[index])
        for index, (source, target) in enumerate(pairs)
    ]
    for copy in copies:
        copy.start()
    for copy in copies:
        copy.wait()


ROUTES = (
    (6, 5, 4, 7, 1, 2, 3, 0),
    (3, 2, 1, 0, 5, 4, 7, 6),
    (1, 6, 7, 2, 0, 3, 5, 4),
    (7, 4, 5, 6, 2, 1, 0, 3),
    (2, 7, 6, 1, 3, 0, 4, 5),
    (4, 0, 3, 5, 7, 6, 1, 2),
    (5, 3, 0, 4, 6, 7, 2, 1),
)


def routes(groups):
    if groups == len(ROUTES[0]):
        found = list(ROUTES)
    else:
        found = [tuple(group ^ step for group in range(groups)) for step in reversed(range(1, groups))]
    return found[:1] + found + [tuple(range(groups))]


def inverse(route):
    return tuple(route.index(group) for group in range(len(route)))


def pick(route, group):
    if len(route) > 8:
        return group ^ route[0]
    code = sum(target << (3 * index) for index, target in enumerate(route))
    return (jnp.int32(code) >> (3 * group)) & 7


def pack_kernel(rep_count, pairs_hbm, strain_hbm, widths_hbm, taps_hbm, *refs):
    out_refs = refs[:-7]
    taps_ref = refs[-7]
    pairs_ref, strain_ref, widths_ref, semaphores, blocks_ref, table_ref = refs[-6:]
    groups = len(out_refs) - 1
    rows, packed = out_refs[0].shape
    listed = pairs_ref.shape[0]
    channels = strain_ref.shape[1]
    members = widths_ref.shape[1]
    fetch(
        [
            (strain_hbm, strain_ref),
            (pairs_hbm, pairs_ref),
            (widths_hbm, widths_ref),
            (taps_hbm, taps_ref),
        ],
        semaphores,
    )
    my_rep = lax.axis_index("rep")
    my_grp = lax.axis_index("grp")

    count = channels // LANES
    filled = strain_ref.shape[0]
    for block in range(count):
        values = strain_ref[:, block * LANES : (block + 1) * LANES].astype(jnp.float32)
        if rows > filled:
            values = jnp.concatenate([values, jnp.zeros((rows - filled, LANES), jnp.float32)], axis=0)
        blocks_ref[block] = values
    blocks_ref[count] = jnp.zeros((rows, LANES), jnp.float32)

    wide = jnp.concatenate(
        [widths_ref[...].astype(jnp.float32), jnp.zeros((1, 2 * LANES - members), jnp.float32)],
        axis=1,
    )
    wide = jnp.broadcast_to(wide, (TILE, 2 * LANES))
    tall = lax.broadcasted_iota(jnp.int32, (TILE, 2 * LANES), 0)
    across = lax.broadcasted_iota(jnp.int32, (TILE, 2 * LANES), 1)
    for member in range(rep_count):
        column = jnp.sum(jnp.where(across == tall + member * TILE, wide, 0.0), axis=1, keepdims=True)
        table_ref[member, :TILE] = jnp.broadcast_to(column, (TILE, LANES))
        table_ref[member, TILE:] = jnp.zeros((rows - TILE, LANES), jnp.float32)

    lane = lax.broadcasted_iota(jnp.int32, (rows, LANES), 1)
    spare = LANES - 8
    for index, (route, out_ref) in enumerate(zip(routes(groups), out_refs)):
        group = pick(route, my_grp)
        tile = group * rep_count + (my_rep & ~1 if index == 1 else my_rep)
        chosen = [tile]
        member, place_of = jnp.int32(0), jnp.int32(-1)
        for slot in range(listed):
            other = pairs_ref[slot, tile]
            chosen.append(jnp.maximum(other, 0))
            among = other - my_grp * rep_count
            inside = (among >= 0) & (among < rep_count)
            member = jnp.where(inside, among, member)
            place_of = jnp.where(inside, slot + 1, place_of)
        own_at = jnp.where(group == my_grp, spare, -1)
        theirs = table_ref[member]
        mine = table_ref[my_rep]
        for block in range(packed // LANES):
            total = jnp.zeros((rows, LANES), jnp.float32)
            for place in range(PER_BLOCK):
                index = block * PER_BLOCK + place
                if index > listed:
                    continue
                start = chosen[index] * TILE
                source = start >> 7
                offset = start & (LANES - 1)
                both = jnp.where(lane >= offset, blocks_ref[source], blocks_ref[source + 1])
                shift = (place * TILE - offset) & (LANES - 1)
                moved = pltpu.roll(both, shift, 1)
                here = (lane >= place * TILE) & (lane < (place + 1) * TILE)
                total = jnp.where(here, moved, total)
            first = block * PER_BLOCK
            here = (place_of >= first) & (place_of < first + PER_BLOCK)
            marked = jnp.where(here, spare + place_of - first, -1)
            total = jnp.where(lane == marked, theirs, total)
            if block == 0:
                total = jnp.where(lane == own_at, mine, total)
            out_ref[:, block * LANES : (block + 1) * LANES] = total.astype(jnp.bfloat16)


def pack(strain, fir_taps, half_widths, pairs, groups, rep_count):
    channels, filled = strain.shape
    rows = max(filled, -(-TILE // 16) * 16)
    tiles, listed = pairs.shape
    members = half_widths.shape[0]
    packed = -(-(listed + 1) // PER_BLOCK) * LANES
    hbm = pl.BlockSpec(memory_space=pltpu.HBM)
    vmem = pl.BlockSpec(memory_space=pltpu.VMEM)
    return pl.pallas_call(
        functools.partial(pack_kernel, rep_count),
        out_shape=[jax.ShapeDtypeStruct((rows, packed), jnp.bfloat16)] * (groups + 1)
        + [jax.ShapeDtypeStruct((1, fir_taps.shape[0]), jnp.float32)],
        in_specs=[hbm] * 4,
        out_specs=[vmem] * (groups + 2),
        scratch_shapes=[
            pltpu.SMEM((listed, tiles), jnp.int32),
            pltpu.VMEM((filled, channels), jnp.bfloat16),
            pltpu.VMEM((1, members), jnp.int32),
            pltpu.SemaphoreType.DMA((4,)),
            pltpu.VMEM((channels // LANES + 1, rows, LANES), jnp.float32),
            pltpu.VMEM((rep_count, rows, LANES), jnp.float32),
        ],
        compiler_params=pltpu.CompilerParams(vmem_limit_bytes=48 * 2**20),
        name="pack",
    )(*[
        pltpu.with_memory_space_constraint(array, pltpu.HBM)
        for array in (pairs.T, strain.T, half_widths[None, :], fir_taps[None, :])
    ])


def split(values):
    high = values.astype(jnp.bfloat16)
    low = (values - high.astype(jnp.float32)).astype(jnp.bfloat16)
    return high, low


def dot(left, right):
    return jnp.dot(left, right, preferred_element_type=jnp.float32)


def condition(period, raw_ref, taps_ref, white_ref):
    groups, rows, packed = raw_ref.shape
    listed = white_ref.shape[0] // TILE - 1
    blocks = packed // LANES
    raw = raw_ref[:, :period, :].astype(jnp.float32).reshape(groups * period, packed)
    samples = jnp.transpose(raw).astype(jnp.bfloat16)
    columns = []
    for block in range(blocks):
        piece = raw_ref[:, :TILE, block * LANES : (block + 1) * LANES].astype(jnp.float32)
        columns.append(jnp.sum(piece, axis=0))

    count = taps_ref.shape[1]
    taps = jnp.concatenate([taps_ref[...], jnp.zeros((1, 2 * LANES - count), jnp.float32)], axis=1)
    bands = pltpu.roll(jnp.broadcast_to(taps, (LANES, 2 * LANES)), 0, 1, stride=1, stride_axis=0)
    parts = []
    empty = jnp.zeros((LANES, LANES), jnp.bfloat16)
    for piece in split(bands):
        near, far = piece[:, :LANES], piece[:, LANES:]
        first = jnp.concatenate([piece, jnp.concatenate([empty, near], axis=1)], axis=0)
        second = jnp.concatenate([far, near], axis=0)
        parts.append((dot(samples[:, : 2 * LANES], first), dot(samples[:, LANES:], second)))
    filtered = jnp.concatenate([parts[0][0] + parts[1][0], parts[0][1] + parts[1][1]], axis=1)

    size = jnp.abs(filtered)
    before = lax.broadcasted_iota(jnp.int32, (2 * LANES, 2 * LANES), 0) <= lax.broadcasted_iota(
        jnp.int32, (2 * LANES, 2 * LANES), 1
    )
    upper = jnp.where(before, 1.0, 0.0).astype(jnp.bfloat16)
    ones = jnp.ones((2 * LANES, LANES), jnp.bfloat16)
    sums = []
    for piece in split(size):
        head, tail = piece[:, : 2 * LANES], piece[:, 2 * LANES :]
        sums.append((dot(head, upper), dot(head, ones), dot(tail, upper[:LANES, :LANES])))
    high, low = sums
    head = high[0] + low[0]
    tail = (high[1] + low[1]) + (high[2] + low[2])
    prefix = [head[:, :LANES], head[:, LANES:], tail]

    lane = lax.broadcasted_iota(jnp.int32, (TILE, LANES), 1)
    for slot in range(listed + 1):
        base = slot // PER_BLOCK * LANES + slot % PER_BLOCK * TILE
        at = slice(base, base + TILE)
        from_lane = LANES - 8 + slot % PER_BLOCK
        column = columns[slot // PER_BLOCK][:, from_lane : from_lane + 1]
        width = jnp.broadcast_to(column, (TILE, LANES))
        whole = width.astype(jnp.int32)
        above = lane + whole
        below = lane - whole - 1
        above_at = above & (LANES - 1)
        below_at = below & (LANES - 1)
        above_by = above >> 7
        below_by = below >> 7
        up = [jnp.take_along_axis(prefix[b][at], above_at, axis=1) for b in range(3)]
        down = [jnp.take_along_axis(prefix[b][at], below_at, axis=1) for b in range(2)]
        full = jnp.broadcast_to(prefix[2][at][:, LANES - 1 :], (TILE, LANES))
        ends = up + [full, full]
        starts = [jnp.zeros((TILE, LANES), jnp.float32)] * 2 + down
        down_last = jnp.take_along_axis(prefix[2][at], below_at, axis=1)
        starts.append(down_last)
        scale = 1.0 / (2.0 * width + 1.0)
        high_0, high_1 = above_by == 0, above_by == 1
        low_0, low_1 = below_by == 0, below_by == -1
        for block in range(3 if slot else 1):
            top = jnp.where(high_0, ends[block], jnp.where(high_1, ends[block + 1], ends[block + 2]))
            low_end = jnp.where(
                low_0, starts[block + 2], jnp.where(low_1, starts[block + 1], starts[block])
            )
            level = (top - low_end) * scale
            value = filtered[at, block * LANES : (block + 1) * LANES] / (level + 1e-05)
            if slot:
                value = jnp.where(width > 0.0, value, 0.0)
            white_ref[slot * TILE : (slot + 1) * TILE, block * LANES : (block + 1) * LANES] = value


def correlate_kernel(period, taps_ref, *refs):
    received = refs[:-11]
    out_hbm, raw_ref, white_ref, partner_ref, reverse_ref = refs[-11:-6]
    low_even, high_even, low_odd, high_odd, packed_ref, semaphores = refs[-6:]
    groups = len(received) - 1
    my_grp = lax.axis_index("grp")
    odd_member = lax.rem(lax.axis_index("rep"), 2) == 1
    for index, (route, ref) in enumerate(zip(routes(groups), received)):
        if index == 0:
            continue
        value = ref[...]
        if index == 1:
            value = jnp.where(odd_member, received[0][...], value)
        raw_ref[pick(inverse(route), my_grp)] = value
    condition(period, raw_ref, taps_ref, white_ref)

    own = white_ref[:TILE, :LANES].astype(jnp.bfloat16)
    row = lax.broadcasted_iota(jnp.int32, (LANES, LANES), 0)
    col = lax.broadcasted_iota(jnp.int32, (LANES, LANES), 1)
    flip = jnp.where(row + col == LANES - 1, 1.0, 0.0).astype(jnp.bfloat16)
    reverse_ref[...] = dot(own, flip)
    partner = white_ref[TILE:, :].astype(jnp.bfloat16)
    rows = partner.shape[0]
    partner_ref[:rows] = partner[:, : 2 * LANES]
    partner_ref[rows:] = partner[:, LANES:]
    listed = rows // TILE
    normalizer = 1.0 / math.sqrt(LANES)
    keep = col <= row
    even, odd = (low_even, high_even), (low_odd, high_odd)
    count = TILE // 8
    parts = 4
    share = listed // parts

    def band(channel):
        line = jnp.broadcast_to(reverse_ref[pl.ds(channel, 1), :], (LANES, LANES))
        turned = pltpu.roll(line, 1, 1, stride=1, stride_axis=0)
        first = jnp.where(keep, turned, 0.0).astype(jnp.bfloat16)
        second = jnp.where(keep, 0.0, turned).astype(jnp.bfloat16)
        return jnp.concatenate([first, second], axis=0)

    def outgoing(group, part):
        tiles = pl.ds(part * share, share)
        return pltpu.make_async_copy(
            packed_ref.at[group, tiles],
            out_hbm.at[0, tiles, :, pl.ds(group * 8, 8), :],
            semaphores.at[group, part],
        )

    def multiply(group, part, held):
        channel = group * 8 + 2 * part
        weights = jnp.concatenate([band(channel), band(channel + 1)], axis=1)
        product = dot(partner_ref[...], weights) * normalizer
        for half, ref in enumerate(held):
            for side in range(2):
                ref[pl.ds(2 * part + side, rows, stride=STRIDE), :] = product[
                    half * rows : (half + 1) * rows, side * LANES : (side + 1) * LANES
                ]

    def convert(group, part, held):
        for tile in range(part * share, (part + 1) * share):
            for line in range(TILE):
                at = pl.ds((tile * TILE + line) * STRIDE, 8)
                both = jnp.concatenate([ref[at, :] for ref in held], axis=1)
                packed_ref[group, tile, line] = both.astype(jnp.bfloat16)

    def together(group, held, before):
        for part in range(parts):
            multiply(group, part, held)
            convert(group - 1, part, before)
            outgoing(group - 1, part).start()

    for part in range(parts):
        multiply(0, part, even)

    def two_groups(index, carry):
        together(2 * index + 1, odd, even)
        together(2 * index + 2, even, odd)
        return carry

    lax.fori_loop(0, count // 2, two_groups, 0)
    for part in range(parts):
        convert(count - 1, part, even)
        outgoing(count - 1, part).start()
    for group in range(count):
        for part in range(parts):
            outgoing(group, part).wait()


def correlate(received, taps, period, listed):
    groups = len(received) - 1
    rows, packed = received[0].shape
    lines = listed * TILE
    vmem = pl.BlockSpec(memory_space=pltpu.VMEM)
    return pl.pallas_call(
        functools.partial(correlate_kernel, period),
        out_shape=jax.ShapeDtypeStruct((1, listed, TILE, TILE, LAGS), jnp.bfloat16),
        in_specs=[vmem] * (len(received) + 1),
        out_specs=pl.BlockSpec(memory_space=pltpu.HBM),
        scratch_shapes=[
            pltpu.VMEM((groups, rows, packed), jnp.bfloat16),
            pltpu.VMEM(((listed + 1) * TILE, groups * period), jnp.float32),
            pltpu.VMEM((2 * lines, 2 * LANES), jnp.bfloat16),
            pltpu.VMEM((TILE, LANES), jnp.float32),
        ]
        + [pltpu.VMEM((lines * STRIDE, LANES), jnp.float32)] * 4
        + [
            pltpu.VMEM((TILE // 8, listed, TILE, 8, LAGS), jnp.bfloat16),
            pltpu.SemaphoreType.DMA((TILE // 8, 4)),
        ],
        compiler_params=pltpu.CompilerParams(vmem_limit_bytes=40 * 2**20),
        name="correlate",
    )(taps, *received)


def on_device(strain, fir_taps, half_widths, pairs):
    groups = lax.axis_size("grp")
    rep_count = lax.axis_size("rep")
    *messages, taps = pack(strain, fir_taps, half_widths, pairs, groups, rep_count)
    received = []
    for index, (route, message) in enumerate(zip(routes(groups), messages)):
        if route != tuple(range(groups)):
            pairs_of = [
                (group * rep_count + member, target * rep_count + member - (index == 1))
                for group, target in enumerate(route)
                for member in range(rep_count)
                if index > 1 or member % 2
            ]
            message = lax.ppermute(message, ("grp", "rep"), pairs_of)
        received.append(message)
    return correlate(received, taps, strain.shape[1], pairs.shape[1])


def solution(mesh):
    placed = (P(None, "grp"), P(), P("grp"), P())
    return jax.shard_map(
        on_device,
        mesh=mesh,
        in_specs=placed,
        out_specs=P(("grp", "rep"), None, None, None, None),
        check_vma=False,
    )
```

```python
import functools
import math

import jax
import jax.numpy as jnp
from jax import lax
from jax.experimental import pallas as pl
from jax.experimental.pallas import tpu as pltpu
from jax.sharding import PartitionSpec as P

TILE = 40
LAGS = 256
LANES = 128
STRIDE = 9
PER_BLOCK = LANES // TILE


def fetch(pairs, semaphores):
    copies = [
        pltpu.make_async_copy(source, target, semaphores.at[index])
        for index, (source, target) in enumerate(pairs)
    ]
    for copy in copies:
        copy.start()
    for copy in copies:
        copy.wait()


ROUTES = (
    ((3, 2, 5, 4, 7, 6, 1, 0), (2, 3, 4, 5, 6, 7, 0, 1), 0),
    ((1, 0, 3, 2, 5, 4, 7, 6), (6, 7, 0, 1, 2, 3, 4, 5), 1),
    ((7, 6, 1, 0, 3, 2, 5, 4), (4, 5, 6, 7, 0, 1, 2, 3), 0),
    ((2, 3, 4, 5, 6, 7, 0, 1), (3, 2, 5, 4, 7, 6, 1, 0), 0),
    ((5, 4, 7, 6, 1, 0, 3, 2), (5, 4, 7, 6, 1, 0, 3, 2), 0),
    ((4, 5, 6, 7, 0, 1, 2, 3), (7, 6, 1, 0, 3, 2, 5, 4), 0),
    ((1, 0, 3, 2, 5, 4, 7, 6), (6, 7, 0, 1, 2, 3, 4, 5), 0),
)


def rounds(groups):
    stay = tuple(range(groups))
    if groups == len(ROUTES[0][0]):
        return list(ROUTES) + [(stay, stay, 0)]
    steps = [tuple(group ^ step for group in range(groups)) for step in reversed(range(groups))]
    return [(route, route, 0) for route in steps]


def goes_to(plan, group, member):
    even, odd, _ = plan
    if even == odd:
        return pick(even, group)
    return jnp.where(lax.rem(member, 2) == 0, pick(even, group), pick(odd, group))


def comes_from(plan, group, member):
    even, odd, crossed = plan
    return goes_to((inverse(even), inverse(odd), 0), group, member ^ crossed)


def inverse(route):
    return tuple(route.index(group) for group in range(len(route)))


def pick(route, group):
    if len(route) > 8:
        return group ^ route[0]
    code = sum(target << (3 * index) for index, target in enumerate(route))
    return (jnp.int32(code) >> (3 * group)) & 7


def pack_kernel(rep_count, pairs_hbm, strain_hbm, widths_hbm, taps_hbm, *refs):
    out_refs = refs[:-7]
    taps_ref = refs[-7]
    pairs_ref, strain_ref, widths_ref, semaphores, blocks_ref, table_ref = refs[-6:]
    groups = len(out_refs)
    rows, packed = out_refs[0].shape
    listed = pairs_ref.shape[0]
    channels = strain_ref.shape[1]
    members = widths_ref.shape[1]
    fetch(
        [
            (strain_hbm, strain_ref),
            (pairs_hbm, pairs_ref),
            (widths_hbm, widths_ref),
            (taps_hbm, taps_ref),
        ],
        semaphores,
    )
    my_rep = lax.axis_index("rep")
    my_grp = lax.axis_index("grp")

    count = channels // LANES
    filled = strain_ref.shape[0]
    for block in range(count):
        values = strain_ref[:, block * LANES : (block + 1) * LANES].astype(jnp.float32)
        if rows > filled:
            values = jnp.concatenate([values, jnp.zeros((rows - filled, LANES), jnp.float32)], axis=0)
        blocks_ref[block] = values
    blocks_ref[count] = jnp.zeros((rows, LANES), jnp.float32)

    wide = jnp.concatenate(
        [widths_ref[...].astype(jnp.float32), jnp.zeros((1, 2 * LANES - members), jnp.float32)],
        axis=1,
    )
    wide = jnp.broadcast_to(wide, (TILE, 2 * LANES))
    tall = lax.broadcasted_iota(jnp.int32, (TILE, 2 * LANES), 0)
    across = lax.broadcasted_iota(jnp.int32, (TILE, 2 * LANES), 1)
    for member in range(rep_count):
        column = jnp.sum(jnp.where(across == tall + member * TILE, wide, 0.0), axis=1, keepdims=True)
        table_ref[member, :TILE] = jnp.broadcast_to(column, (TILE, LANES))
        table_ref[member, TILE:] = jnp.zeros((rows - TILE, LANES), jnp.float32)

    lane = lax.broadcasted_iota(jnp.int32, (rows, LANES), 1)
    spare = LANES - 8
    for plan, out_ref in zip(rounds(groups), out_refs):
        group = goes_to(plan, my_grp, my_rep)
        tile = group * rep_count + (my_rep ^ plan[2])
        chosen = [tile]
        member, place_of = jnp.int32(0), jnp.int32(-1)
        for slot in range(listed):
            other = pairs_ref[slot, tile]
            chosen.append(jnp.maximum(other, 0))
            among = other - my_grp * rep_count
            inside = (among >= 0) & (among < rep_count)
            member = jnp.where(inside, among, member)
            place_of = jnp.where(inside, slot + 1, place_of)
        own_at = jnp.where(group == my_grp, spare, -1)
        theirs = table_ref[member]
        mine = table_ref[my_rep]
        for block in range(packed // LANES):
            total = jnp.zeros((rows, LANES), jnp.float32)
            for place in range(PER_BLOCK):
                index = block * PER_BLOCK + place
                if index > listed:
                    continue
                start = chosen[index] * TILE
                source = start >> 7
                offset = start & (LANES - 1)
                both = jnp.where(lane >= offset, blocks_ref[source], blocks_ref[source + 1])
                shift = (place * TILE - offset) & (LANES - 1)
                moved = pltpu.roll(both, shift, 1)
                here = (lane >= place * TILE) & (lane < (place + 1) * TILE)
                total = jnp.where(here, moved, total)
            first = block * PER_BLOCK
            here = (place_of >= first) & (place_of < first + PER_BLOCK)
            marked = jnp.where(here, spare + place_of - first, -1)
            total = jnp.where(lane == marked, theirs, total)
            if block == 0:
                total = jnp.where(lane == own_at, mine, total)
            out_ref[:, block * LANES : (block + 1) * LANES] = total.astype(jnp.bfloat16)


def pack(strain, fir_taps, half_widths, pairs, groups, rep_count):
    channels, filled = strain.shape
    rows = max(filled, -(-TILE // 16) * 16)
    tiles, listed = pairs.shape
    members = half_widths.shape[0]
    packed = -(-(listed + 1) // PER_BLOCK) * LANES
    hbm = pl.BlockSpec(memory_space=pltpu.HBM)
    vmem = pl.BlockSpec(memory_space=pltpu.VMEM)
    return pl.pallas_call(
        functools.partial(pack_kernel, rep_count),
        out_shape=[jax.ShapeDtypeStruct((rows, packed), jnp.bfloat16)] * groups
        + [jax.ShapeDtypeStruct((1, fir_taps.shape[0]), jnp.float32)],
        in_specs=[hbm] * 4,
        out_specs=[vmem] * (groups + 1),
        scratch_shapes=[
            pltpu.SMEM((listed, tiles), jnp.int32),
            pltpu.VMEM((filled, channels), jnp.bfloat16),
            pltpu.VMEM((1, members), jnp.int32),
            pltpu.SemaphoreType.DMA((4,)),
            pltpu.VMEM((channels // LANES + 1, rows, LANES), jnp.float32),
            pltpu.VMEM((rep_count, rows, LANES), jnp.float32),
        ],
        compiler_params=pltpu.CompilerParams(vmem_limit_bytes=48 * 2**20),
        name="pack",
    )(*[
        pltpu.with_memory_space_constraint(array, pltpu.HBM)
        for array in (pairs.T, strain.T, half_widths[None, :], fir_taps[None, :])
    ])


def split(values):
    high = values.astype(jnp.bfloat16)
    low = (values - high.astype(jnp.float32)).astype(jnp.bfloat16)
    return high, low


def dot(left, right):
    return jnp.dot(left, right, preferred_element_type=jnp.float32)


def condition(period, raw_ref, taps_ref, white_ref):
    groups, rows, packed = raw_ref.shape
    listed = white_ref.shape[0] // TILE - 1
    blocks = packed // LANES
    raw = raw_ref[:, :period, :].reshape(groups * period, packed)
    same = lax.broadcasted_iota(jnp.int32, (LANES, LANES), 0) == lax.broadcasted_iota(
        jnp.int32, (LANES, LANES), 1
    )
    identity = jnp.where(same, 1.0, 0.0).astype(jnp.bfloat16)
    turned = [
        lax.dot_general(
            identity,
            raw[:, block * LANES : (block + 1) * LANES],
            (((1,), (1,)), ((), ())),
            preferred_element_type=jnp.float32,
        ).astype(jnp.bfloat16)
        for block in range(blocks)
    ]
    samples = jnp.concatenate(turned, axis=0)
    columns = []
    for block in range(blocks):
        piece = raw_ref[:, :TILE, block * LANES : (block + 1) * LANES].astype(jnp.float32)
        columns.append(jnp.sum(piece, axis=0))

    count = taps_ref.shape[1]
    taps = jnp.concatenate([taps_ref[...], jnp.zeros((1, 2 * LANES - count), jnp.float32)], axis=1)
    bands = pltpu.roll(jnp.broadcast_to(taps, (LANES, 2 * LANES)), 0, 1, stride=1, stride_axis=0)
    parts = []
    empty = jnp.zeros((LANES, LANES), jnp.bfloat16)
    for piece in split(bands):
        near, far = piece[:, :LANES], piece[:, LANES:]
        first = jnp.concatenate([piece, jnp.concatenate([empty, near], axis=1)], axis=0)
        second = jnp.concatenate([far, near], axis=0)
        parts.append((dot(samples[:, : 2 * LANES], first), dot(samples[:, LANES:], second)))
    filtered = jnp.concatenate([parts[0][0] + parts[1][0], parts[0][1] + parts[1][1]], axis=1)

    size = jnp.abs(filtered)
    before = lax.broadcasted_iota(jnp.int32, (2 * LANES, 2 * LANES), 0) <= lax.broadcasted_iota(
        jnp.int32, (2 * LANES, 2 * LANES), 1
    )
    upper = jnp.where(before, 1.0, 0.0).astype(jnp.bfloat16)
    ones = jnp.ones((2 * LANES, LANES), jnp.bfloat16)
    sums = []
    for piece in split(size):
        head, tail = piece[:, : 2 * LANES], piece[:, 2 * LANES :]
        sums.append((dot(head, upper), dot(head, ones), dot(tail, upper[:LANES, :LANES])))
    high, low = sums
    head = high[0] + low[0]
    tail = (high[1] + low[1]) + (high[2] + low[2])
    prefix = [head[:, :LANES], head[:, LANES:], tail]

    lane = lax.broadcasted_iota(jnp.int32, (TILE, LANES), 1)
    for slot in range(listed + 1):
        base = slot // PER_BLOCK * LANES + slot % PER_BLOCK * TILE
        at = slice(base, base + TILE)
        from_lane = LANES - 8 + slot % PER_BLOCK
        column = columns[slot // PER_BLOCK][:, from_lane : from_lane + 1]
        width = jnp.broadcast_to(column, (TILE, LANES))
        whole = width.astype(jnp.int32)
        above = lane + whole
        below = lane - whole - 1
        above_at = above & (LANES - 1)
        below_at = below & (LANES - 1)
        above_by = above >> 7
        below_by = below >> 7
        up = [jnp.take_along_axis(prefix[b][at], above_at, axis=1) for b in range(3)]
        down = [jnp.take_along_axis(prefix[b][at], below_at, axis=1) for b in range(2)]
        full = jnp.broadcast_to(prefix[2][at][:, LANES - 1 :], (TILE, LANES))
        ends = up + [full, full]
        starts = [jnp.zeros((TILE, LANES), jnp.float32)] * 2 + down
        down_last = jnp.take_along_axis(prefix[2][at], below_at, axis=1)
        starts.append(down_last)
        scale = 1.0 / (2.0 * width + 1.0)
        high_0, high_1 = above_by == 0, above_by == 1
        low_0, low_1 = below_by == 0, below_by == -1
        for block in range(3 if slot else 1):
            top = jnp.where(high_0, ends[block], jnp.where(high_1, ends[block + 1], ends[block + 2]))
            low_end = jnp.where(
                low_0, starts[block + 2], jnp.where(low_1, starts[block + 1], starts[block])
            )
            level = (top - low_end) * scale
            value = filtered[at, block * LANES : (block + 1) * LANES] / (level + 1e-05)
            if slot:
                value = jnp.where(width > 0.0, value, 0.0)
            white_ref[slot * TILE : (slot + 1) * TILE, block * LANES : (block + 1) * LANES] = value


def correlate_kernel(period, taps_ref, *refs):
    received = refs[:-11]
    out_hbm, raw_ref, white_ref, partner_ref, reverse_ref = refs[-11:-6]
    low_even, high_even, low_odd, high_odd, packed_ref, semaphores = refs[-6:]
    groups = len(received)
    my_grp = lax.axis_index("grp")
    my_rep = lax.axis_index("rep")
    for plan, ref in zip(rounds(groups), received):
        raw_ref[comes_from(plan, my_grp, my_rep)] = ref[...]
    condition(period, raw_ref, taps_ref, white_ref)

    own = white_ref[:TILE, :LANES].astype(jnp.bfloat16)
    row = lax.broadcasted_iota(jnp.int32, (LANES, LANES), 0)
    col = lax.broadcasted_iota(jnp.int32, (LANES, LANES), 1)
    flip = jnp.where(row + col == LANES - 1, 1.0, 0.0).astype(jnp.bfloat16)
    reverse_ref[...] = dot(own, flip)
    partner = white_ref[TILE:, :].astype(jnp.bfloat16)
    rows = partner.shape[0]
    partner_ref[:rows] = partner[:, : 2 * LANES]
    partner_ref[rows:] = partner[:, LANES:]
    listed = rows // TILE
    normalizer = 1.0 / math.sqrt(LANES)
    keep = col <= row
    even, odd = (low_even, high_even), (low_odd, high_odd)
    count = TILE // 8
    parts = 4
    share = listed // parts

    def band(channel):
        line = jnp.broadcast_to(reverse_ref[pl.ds(channel, 1), :], (LANES, LANES))
        turned = pltpu.roll(line, 1, 1, stride=1, stride_axis=0)
        first = jnp.where(keep, turned, 0.0).astype(jnp.bfloat16)
        second = jnp.where(keep, 0.0, turned).astype(jnp.bfloat16)
        return jnp.concatenate([first, second], axis=0)

    def outgoing(group, part):
        tiles = pl.ds(part * share, share)
        return pltpu.make_async_copy(
            packed_ref.at[group, tiles],
            out_hbm.at[0, tiles, :, pl.ds(group * 8, 8), :],
            semaphores.at[group, part],
        )

    def multiply(group, part, held):
        channel = group * 8 + 2 * part
        weights = jnp.concatenate([band(channel), band(channel + 1)], axis=1)
        product = dot(partner_ref[...], weights) * normalizer
        for half, ref in enumerate(held):
            for side in range(2):
                ref[pl.ds(2 * part + side, rows, stride=STRIDE), :] = product[
                    half * rows : (half + 1) * rows, side * LANES : (side + 1) * LANES
                ]

    def convert(group, part, held):
        for tile in range(part * share, (part + 1) * share):
            for line in range(TILE):
                at = pl.ds((tile * TILE + line) * STRIDE, 8)
                both = jnp.concatenate([ref[at, :] for ref in held], axis=1)
                packed_ref[group, tile, line] = both.astype(jnp.bfloat16)

    def together(group, held, before):
        for part in range(parts):
            multiply(group, part, held)
            convert(group - 1, part, before)
            outgoing(group - 1, part).start()

    for part in range(parts):
        multiply(0, part, even)

    def two_groups(index, carry):
        together(2 * index + 1, odd, even)
        together(2 * index + 2, even, odd)
        return carry

    lax.fori_loop(0, count // 2, two_groups, 0)
    for part in range(parts):
        convert(count - 1, part, even)
        outgoing(count - 1, part).start()
    for group in range(count):
        for part in range(parts):
            outgoing(group, part).wait()


def correlate(received, taps, period, listed):
    groups = len(received)
    rows, packed = received[0].shape
    lines = listed * TILE
    vmem = pl.BlockSpec(memory_space=pltpu.VMEM)
    return pl.pallas_call(
        functools.partial(correlate_kernel, period),
        out_shape=jax.ShapeDtypeStruct((1, listed, TILE, TILE, LAGS), jnp.bfloat16),
        in_specs=[vmem] * (groups + 1),
        out_specs=pl.BlockSpec(memory_space=pltpu.HBM),
        scratch_shapes=[
            pltpu.VMEM((groups, rows, packed), jnp.bfloat16),
            pltpu.VMEM(((listed + 1) * TILE, groups * period), jnp.float32),
            pltpu.VMEM((2 * lines, 2 * LANES), jnp.bfloat16),
            pltpu.VMEM((TILE, LANES), jnp.float32),
        ]
        + [pltpu.VMEM((lines * STRIDE, LANES), jnp.float32)] * 4
        + [
            pltpu.VMEM((TILE // 8, listed, TILE, 8, LAGS), jnp.bfloat16),
            pltpu.SemaphoreType.DMA((TILE // 8, 4)),
        ],
        compiler_params=pltpu.CompilerParams(vmem_limit_bytes=40 * 2**20),
        name="correlate",
    )(taps, *received)


def on_device(strain, fir_taps, half_widths, pairs):
    groups = lax.axis_size("grp")
    rep_count = lax.axis_size("rep")
    *messages, taps = pack(strain, fir_taps, half_widths, pairs, groups, rep_count)
    received = []
    for plan, message in zip(rounds(groups), messages):
        if plan[0] != tuple(range(groups)):
            way = [
                (group * rep_count + member, plan[member % 2][group] * rep_count + (member ^ plan[2]))
                for group in range(groups)
                for member in range(rep_count)
            ]
            message = lax.ppermute(message, ("grp", "rep"), way)
        received.append(message)
    return correlate(received, taps, strain.shape[1], pairs.shape[1])


def solution(mesh):
    placed = (P(None, "grp"), P(), P("grp"), P())
    return jax.shard_map(
        on_device,
        mesh=mesh,
        in_specs=placed,
        out_specs=P(("grp", "rep"), None, None, None, None),
        check_vma=False,
    )
```

```python
import functools
import math

import jax
import jax.numpy as jnp
from jax import lax
from jax.experimental import pallas as pl
from jax.experimental.pallas import tpu as pltpu
from jax.sharding import PartitionSpec as P

TILE = 40
LAGS = 256
LANES = 128
STRIDE = 9
PER_BLOCK = LANES // TILE


def fetch(pairs, semaphores):
    copies = [
        pltpu.make_async_copy(source, target, semaphores.at[index])
        for index, (source, target) in enumerate(pairs)
    ]
    for copy in copies:
        copy.start()
    for copy in copies:
        copy.wait()


ROUTES = (
    ((3, 2, 5, 4, 7, 6, 1, 0), (2, 3, 4, 5, 6, 7, 0, 1), 0),
    ((1, 0, 3, 2, 5, 4, 7, 6), (6, 7, 0, 1, 2, 3, 4, 5), 1),
    ((7, 6, 1, 0, 3, 2, 5, 4), (4, 5, 6, 7, 0, 1, 2, 3), 0),
    ((2, 3, 4, 5, 6, 7, 0, 1), (3, 2, 5, 4, 7, 6, 1, 0), 0),
    ((5, 4, 7, 6, 1, 0, 3, 2), (5, 4, 7, 6, 1, 0, 3, 2), 0),
    ((4, 5, 6, 7, 0, 1, 2, 3), (7, 6, 1, 0, 3, 2, 5, 4), 0),
    ((1, 0, 3, 2, 5, 4, 7, 6), (6, 7, 0, 1, 2, 3, 4, 5), 0),
)


def rounds(groups):
    stay = tuple(range(groups))
    if groups == len(ROUTES[0][0]):
        return list(ROUTES) + [(stay, stay, 0)]
    steps = [tuple(group ^ step for group in range(groups)) for step in reversed(range(groups))]
    return [(route, route, 0) for route in steps]


def goes_to(plan, group, member):
    even, odd, _ = plan
    if even == odd:
        return pick(even, group)
    return jnp.where(lax.rem(member, 2) == 0, pick(even, group), pick(odd, group))


def comes_from(plan, group, member):
    even, odd, crossed = plan
    return goes_to((inverse(even), inverse(odd), 0), group, member ^ crossed)


def inverse(route):
    return tuple(route.index(group) for group in range(len(route)))


def pick(route, group):
    if len(route) > 8:
        return group ^ route[0]
    code = sum(target << (3 * index) for index, target in enumerate(route))
    return (jnp.int32(code) >> (3 * group)) & 7


def pack_kernel(rep_count, pairs_hbm, strain_hbm, widths_hbm, taps_hbm, *refs):
    out_refs = refs[:-7]
    taps_ref = refs[-7]
    pairs_ref, strain_ref, widths_ref, semaphores, blocks_ref, table_ref = refs[-6:]
    groups = len(out_refs)
    rows, packed = out_refs[0].shape
    listed = pairs_ref.shape[0]
    channels = strain_ref.shape[1]
    members = widths_ref.shape[1]
    fetch(
        [
            (strain_hbm, strain_ref),
            (pairs_hbm, pairs_ref),
            (widths_hbm, widths_ref),
            (taps_hbm, taps_ref),
        ],
        semaphores,
    )
    my_rep = lax.axis_index("rep")
    my_grp = lax.axis_index("grp")

    count = channels // LANES
    filled = strain_ref.shape[0]
    for block in range(count):
        values = strain_ref[:, block * LANES : (block + 1) * LANES].astype(jnp.float32)
        if rows > filled:
            values = jnp.concatenate([values, jnp.zeros((rows - filled, LANES), jnp.float32)], axis=0)
        blocks_ref[block] = values
    blocks_ref[count] = jnp.zeros((rows, LANES), jnp.float32)

    wide = jnp.concatenate(
        [widths_ref[...].astype(jnp.float32), jnp.zeros((1, 2 * LANES - members), jnp.float32)],
        axis=1,
    )
    wide = jnp.broadcast_to(wide, (TILE, 2 * LANES))
    tall = lax.broadcasted_iota(jnp.int32, (TILE, 2 * LANES), 0)
    across = lax.broadcasted_iota(jnp.int32, (TILE, 2 * LANES), 1)
    for member in range(rep_count):
        column = jnp.sum(jnp.where(across == tall + member * TILE, wide, 0.0), axis=1, keepdims=True)
        table_ref[member, :TILE] = jnp.broadcast_to(column, (TILE, LANES))
        table_ref[member, TILE:] = jnp.zeros((rows - TILE, LANES), jnp.float32)

    lane = lax.broadcasted_iota(jnp.int32, (rows, LANES), 1)
    spare = LANES - 8
    for plan, out_ref in zip(rounds(groups), out_refs):
        group = goes_to(plan, my_grp, my_rep)
        tile = group * rep_count + (my_rep ^ plan[2])
        chosen = [tile]
        member, place_of = jnp.int32(0), jnp.int32(-1)
        for slot in range(listed):
            other = pairs_ref[slot, tile]
            chosen.append(jnp.maximum(other, 0))
            among = other - my_grp * rep_count
            inside = (among >= 0) & (among < rep_count)
            member = jnp.where(inside, among, member)
            place_of = jnp.where(inside, slot + 1, place_of)
        own_at = jnp.where(group == my_grp, spare, -1)
        theirs = table_ref[member]
        mine = table_ref[my_rep]
        for block in range(packed // LANES):
            total = jnp.zeros((rows, LANES), jnp.float32)
            for place in range(PER_BLOCK):
                index = block * PER_BLOCK + place
                if index > listed:
                    continue
                start = chosen[index] * TILE
                source = start >> 7
                offset = start & (LANES - 1)
                both = jnp.where(lane >= offset, blocks_ref[source], blocks_ref[source + 1])
                shift = (place * TILE - offset) & (LANES - 1)
                moved = pltpu.roll(both, shift, 1)
                here = (lane >= place * TILE) & (lane < (place + 1) * TILE)
                total = jnp.where(here, moved, total)
            first = block * PER_BLOCK
            here = (place_of >= first) & (place_of < first + PER_BLOCK)
            marked = jnp.where(here, spare + place_of - first, -1)
            total = jnp.where(lane == marked, theirs, total)
            if block == 0:
                total = jnp.where(lane == own_at, mine, total)
            out_ref[:, block * LANES : (block + 1) * LANES] = total.astype(jnp.bfloat16)


def pack(strain, fir_taps, half_widths, pairs, groups, rep_count):
    channels, filled = strain.shape
    rows = max(filled, -(-TILE // 16) * 16)
    tiles, listed = pairs.shape
    members = half_widths.shape[0]
    packed = -(-(listed + 1) // PER_BLOCK) * LANES
    hbm = pl.BlockSpec(memory_space=pltpu.HBM)
    vmem = pl.BlockSpec(memory_space=pltpu.VMEM)
    return pl.pallas_call(
        functools.partial(pack_kernel, rep_count),
        out_shape=[jax.ShapeDtypeStruct((rows, packed), jnp.bfloat16)] * groups
        + [jax.ShapeDtypeStruct((1, fir_taps.shape[0]), jnp.float32)],
        in_specs=[hbm] * 4,
        out_specs=[vmem] * (groups + 1),
        scratch_shapes=[
            pltpu.SMEM((listed, tiles), jnp.int32),
            pltpu.VMEM((filled, channels), jnp.bfloat16),
            pltpu.VMEM((1, members), jnp.int32),
            pltpu.SemaphoreType.DMA((4,)),
            pltpu.VMEM((channels // LANES + 1, rows, LANES), jnp.float32),
            pltpu.VMEM((rep_count, rows, LANES), jnp.float32),
        ],
        compiler_params=pltpu.CompilerParams(vmem_limit_bytes=48 * 2**20),
        name="pack",
    )(*[
        pltpu.with_memory_space_constraint(array, pltpu.HBM)
        for array in (pairs.T, strain.T, half_widths[None, :], fir_taps[None, :])
    ])


def split(values):
    high = values.astype(jnp.bfloat16)
    low = (values - high.astype(jnp.float32)).astype(jnp.bfloat16)
    return high, low


def dot(left, right):
    return jnp.dot(left, right, preferred_element_type=jnp.float32)


def condition(period, raw_ref, taps_ref, white_ref):
    groups, rows, packed = raw_ref.shape
    listed = white_ref.shape[0] // TILE - 1
    blocks = packed // LANES
    raw = raw_ref[:, :period, :].astype(jnp.float32).reshape(groups * period, packed)
    samples = jnp.transpose(raw).astype(jnp.bfloat16)
    columns = []
    for block in range(blocks):
        piece = raw_ref[:, :TILE, block * LANES : (block + 1) * LANES].astype(jnp.float32)
        columns.append(jnp.sum(piece, axis=0))

    count = taps_ref.shape[1]
    taps = jnp.concatenate([taps_ref[...], jnp.zeros((1, 2 * LANES - count), jnp.float32)], axis=1)
    bands = pltpu.roll(jnp.broadcast_to(taps, (LANES, 2 * LANES)), 0, 1, stride=1, stride_axis=0)
    parts = []
    empty = jnp.zeros((LANES, LANES), jnp.bfloat16)
    for piece in split(bands):
        near, far = piece[:, :LANES], piece[:, LANES:]
        first = jnp.concatenate([piece, jnp.concatenate([empty, near], axis=1)], axis=0)
        second = jnp.concatenate([far, near], axis=0)
        parts.append((dot(samples[:, : 2 * LANES], first), dot(samples[:, LANES:], second)))
    filtered = jnp.concatenate([parts[0][0] + parts[1][0], parts[0][1] + parts[1][1]], axis=1)

    size = jnp.abs(filtered)
    before = lax.broadcasted_iota(jnp.int32, (2 * LANES, 2 * LANES), 0) <= lax.broadcasted_iota(
        jnp.int32, (2 * LANES, 2 * LANES), 1
    )
    upper = jnp.where(before, 1.0, 0.0).astype(jnp.bfloat16)
    ones = jnp.ones((2 * LANES, LANES), jnp.bfloat16)
    sums = []
    for piece in split(size):
        head, tail = piece[:, : 2 * LANES], piece[:, 2 * LANES :]
        sums.append((dot(head, upper), dot(head, ones), dot(tail, upper[:LANES, :LANES])))
    high, low = sums
    head = high[0] + low[0]
    tail = (high[1] + low[1]) + (high[2] + low[2])
    prefix = [head[:, :LANES], head[:, LANES:], tail]

    lane = lax.broadcasted_iota(jnp.int32, (TILE, LANES), 1)
    for slot in range(listed + 1):
        base = slot // PER_BLOCK * LANES + slot % PER_BLOCK * TILE
        at = slice(base, base + TILE)
        from_lane = LANES - 8 + slot % PER_BLOCK
        column = columns[slot // PER_BLOCK][:, from_lane : from_lane + 1]
        width = jnp.broadcast_to(column, (TILE, LANES))
        whole = width.astype(jnp.int32)
        above = lane + whole
        below = lane - whole - 1
        above_at = above & (LANES - 1)
        below_at = below & (LANES - 1)
        above_by = above >> 7
        below_by = below >> 7
        up = [jnp.take_along_axis(prefix[b][at], above_at, axis=1) for b in range(3)]
        down = [jnp.take_along_axis(prefix[b][at], below_at, axis=1) for b in range(2)]
        full = jnp.broadcast_to(prefix[2][at][:, LANES - 1 :], (TILE, LANES))
        ends = up + [full, full]
        starts = [jnp.zeros((TILE, LANES), jnp.float32)] * 2 + down
        down_last = jnp.take_along_axis(prefix[2][at], below_at, axis=1)
        starts.append(down_last)
        scale = 1.0 / (2.0 * width + 1.0)
        high_0, high_1 = above_by == 0, above_by == 1
        low_0, low_1 = below_by == 0, below_by == -1
        for block in range(3 if slot else 1):
            top = jnp.where(high_0, ends[block], jnp.where(high_1, ends[block + 1], ends[block + 2]))
            low_end = jnp.where(
                low_0, starts[block + 2], jnp.where(low_1, starts[block + 1], starts[block])
            )
            level = (top - low_end) * scale
            value = filtered[at, block * LANES : (block + 1) * LANES] / (level + 1e-05)
            if slot:
                value = jnp.where(width > 0.0, value, 0.0)
            white_ref[slot * TILE : (slot + 1) * TILE, block * LANES : (block + 1) * LANES] = value


def correlate_kernel(period, taps_ref, *refs):
    received = refs[:-11]
    out_hbm, raw_ref, white_ref, partner_ref, reverse_ref = refs[-11:-6]
    low_even, high_even, low_odd, high_odd, packed_ref, semaphores = refs[-6:]
    groups = len(received)
    my_grp = lax.axis_index("grp")
    my_rep = lax.axis_index("rep")
    for plan, ref in zip(rounds(groups), received):
        raw_ref[comes_from(plan, my_grp, my_rep)] = ref[...]
    condition(period, raw_ref, taps_ref, white_ref)

    own = white_ref[:TILE, :LANES].astype(jnp.bfloat16)
    row = lax.broadcasted_iota(jnp.int32, (LANES, LANES), 0)
    col = lax.broadcasted_iota(jnp.int32, (LANES, LANES), 1)
    flip = jnp.where(row + col == LANES - 1, 1.0, 0.0).astype(jnp.bfloat16)
    reverse_ref[...] = dot(own, flip)
    partner = white_ref[TILE:, :].astype(jnp.bfloat16)
    rows = partner.shape[0]
    partner_ref[:rows] = partner[:, : 2 * LANES]
    partner_ref[rows:] = partner[:, LANES:]
    listed = rows // TILE
    normalizer = 1.0 / math.sqrt(LANES)
    keep = col <= row
    even, odd = (low_even, high_even), (low_odd, high_odd)
    count = TILE // 8
    parts = 4
    share = listed // parts

    def band(channel):
        line = jnp.broadcast_to(reverse_ref[pl.ds(channel, 1), :], (LANES, LANES))
        turned = pltpu.roll(line, 1, 1, stride=1, stride_axis=0)
        first = jnp.where(keep, turned, 0.0).astype(jnp.bfloat16)
        second = jnp.where(keep, 0.0, turned).astype(jnp.bfloat16)
        return jnp.concatenate([first, second], axis=0)

    def outgoing(group, part):
        tiles = pl.ds(part * share, share)
        return pltpu.make_async_copy(
            packed_ref.at[group, tiles],
            out_hbm.at[0, tiles, :, pl.ds(group * 8, 8), :],
            semaphores.at[group, part],
        )

    wide = 4

    def multiply(group, part, held):
        channel = group * 8 + wide * part
        weights = jnp.concatenate([band(channel + side) for side in range(wide)], axis=1)
        product = dot(partner_ref[...], weights) * normalizer
        for half, ref in enumerate(held):
            for side in range(wide):
                ref[pl.ds(wide * part + side, rows, stride=STRIDE), :] = product[
                    half * rows : (half + 1) * rows, side * LANES : (side + 1) * LANES
                ]

    def convert(group, part, held):
        for tile in range(part * share, (part + 1) * share):
            for line in range(TILE):
                at = pl.ds((tile * TILE + line) * STRIDE, 8)
                both = jnp.concatenate([ref[at, :] for ref in held], axis=1)
                packed_ref[group, tile, line] = both.astype(jnp.bfloat16)

    def together(group, held, before):
        for part in range(parts):
            if part % 2 == 0:
                multiply(group, part // 2, held)
            convert(group - 1, part, before)
            outgoing(group - 1, part).start()

    for part in range(8 // wide):
        multiply(0, part, even)

    def two_groups(index, carry):
        together(2 * index + 1, odd, even)
        together(2 * index + 2, even, odd)
        return carry

    lax.fori_loop(0, count // 2, two_groups, 0)
    for part in range(parts):
        convert(count - 1, part, even)
        outgoing(count - 1, part).start()
    for group in range(count):
        for part in range(parts):
            outgoing(group, part).wait()


def correlate(received, taps, period, listed):
    groups = len(received)
    rows, packed = received[0].shape
    lines = listed * TILE
    vmem = pl.BlockSpec(memory_space=pltpu.VMEM)
    return pl.pallas_call(
        functools.partial(correlate_kernel, period),
        out_shape=jax.ShapeDtypeStruct((1, listed, TILE, TILE, LAGS), jnp.bfloat16),
        in_specs=[vmem] * (groups + 1),
        out_specs=pl.BlockSpec(memory_space=pltpu.HBM),
        scratch_shapes=[
            pltpu.VMEM((groups, rows, packed), jnp.bfloat16),
            pltpu.VMEM(((listed + 1) * TILE, groups * period), jnp.float32),
            pltpu.VMEM((2 * lines, 2 * LANES), jnp.bfloat16),
            pltpu.VMEM((TILE, LANES), jnp.float32),
        ]
        + [pltpu.VMEM((lines * STRIDE, LANES), jnp.float32)] * 4
        + [
            pltpu.VMEM((TILE // 8, listed, TILE, 8, LAGS), jnp.bfloat16),
            pltpu.SemaphoreType.DMA((TILE // 8, 4)),
        ],
        compiler_params=pltpu.CompilerParams(vmem_limit_bytes=40 * 2**20),
        name="correlate",
    )(taps, *received)


def on_device(strain, fir_taps, half_widths, pairs):
    groups = lax.axis_size("grp")
    rep_count = lax.axis_size("rep")
    *messages, taps = pack(strain, fir_taps, half_widths, pairs, groups, rep_count)
    received = []
    for plan, message in zip(rounds(groups), messages):
        if plan[0] != tuple(range(groups)):
            way = [
                (group * rep_count + member, plan[member % 2][group] * rep_count + (member ^ plan[2]))
                for group in range(groups)
                for member in range(rep_count)
            ]
            message = lax.ppermute(message, ("grp", "rep"), way)
        received.append(message)
    return correlate(received, taps, strain.shape[1], pairs.shape[1])


def solution(mesh):
    placed = (P(None, "grp"), P(), P("grp"), P())
    return jax.shard_map(
        on_device,
        mesh=mesh,
        in_specs=placed,
        out_specs=P(("grp", "rep"), None, None, None, None),
        check_vma=False,
    )
```

```python
import functools
import math

import jax
import jax.numpy as jnp
from jax import lax
from jax.experimental import pallas as pl
from jax.experimental.pallas import tpu as pltpu
from jax.sharding import PartitionSpec as P

TILE = 40
LAGS = 256
LANES = 128
STRIDE = 9
PER_BLOCK = LANES // TILE


def fetch(pairs, semaphores):
    copies = [
        pltpu.make_async_copy(source, target, semaphores.at[index])
        for index, (source, target) in enumerate(pairs)
    ]
    for copy in copies:
        copy.start()
    for copy in copies:
        copy.wait()


ROUTES = (
    ((3, 2, 5, 4, 7, 6, 1, 0), (2, 3, 4, 5, 6, 7, 0, 1), 0),
    ((1, 0, 3, 2, 5, 4, 7, 6), (6, 7, 0, 1, 2, 3, 4, 5), 1),
    ((7, 6, 1, 0, 3, 2, 5, 4), (4, 5, 6, 7, 0, 1, 2, 3), 0),
    ((2, 3, 4, 5, 6, 7, 0, 1), (3, 2, 5, 4, 7, 6, 1, 0), 0),
    ((5, 4, 7, 6, 1, 0, 3, 2), (5, 4, 7, 6, 1, 0, 3, 2), 0),
    ((4, 5, 6, 7, 0, 1, 2, 3), (7, 6, 1, 0, 3, 2, 5, 4), 0),
    ((1, 0, 3, 2, 5, 4, 7, 6), (6, 7, 0, 1, 2, 3, 4, 5), 0),
)


def rounds(groups):
    stay = tuple(range(groups))
    if groups == len(ROUTES[0][0]):
        return list(ROUTES) + [(stay, stay, 0)]
    steps = [tuple(group ^ step for group in range(groups)) for step in reversed(range(groups))]
    return [(route, route, 0) for route in steps]


def goes_to(plan, group, member):
    even, odd, _ = plan
    if even == odd:
        return pick(even, group)
    return jnp.where(lax.rem(member, 2) == 0, pick(even, group), pick(odd, group))


def comes_from(plan, group, member):
    even, odd, crossed = plan
    return goes_to((inverse(even), inverse(odd), 0), group, member ^ crossed)


def inverse(route):
    return tuple(route.index(group) for group in range(len(route)))


def pick(route, group):
    if len(route) > 8:
        return group ^ route[0]
    code = sum(target << (3 * index) for index, target in enumerate(route))
    return (jnp.int32(code) >> (3 * group)) & 7


def pack_kernel(rep_count, pairs_hbm, strain_hbm, widths_hbm, taps_hbm, *refs):
    out_refs = refs[:-7]
    taps_ref = refs[-7]
    pairs_ref, strain_ref, widths_ref, semaphores, blocks_ref, table_ref = refs[-6:]
    groups = len(out_refs)
    rows, packed = out_refs[0].shape
    listed = pairs_ref.shape[0]
    channels = strain_ref.shape[1]
    members = widths_ref.shape[1]
    fetch(
        [
            (strain_hbm, strain_ref),
            (pairs_hbm, pairs_ref),
            (widths_hbm, widths_ref),
            (taps_hbm, taps_ref),
        ],
        semaphores,
    )
    my_rep = lax.axis_index("rep")
    my_grp = lax.axis_index("grp")

    count = channels // LANES
    filled = strain_ref.shape[0]
    for block in range(count):
        values = strain_ref[:, block * LANES : (block + 1) * LANES].astype(jnp.float32)
        if rows > filled:
            values = jnp.concatenate([values, jnp.zeros((rows - filled, LANES), jnp.float32)], axis=0)
        blocks_ref[block] = values
    blocks_ref[count] = jnp.zeros((rows, LANES), jnp.float32)

    wide = jnp.concatenate(
        [widths_ref[...].astype(jnp.float32), jnp.zeros((1, 2 * LANES - members), jnp.float32)],
        axis=1,
    )
    wide = jnp.broadcast_to(wide, (TILE, 2 * LANES))
    tall = lax.broadcasted_iota(jnp.int32, (TILE, 2 * LANES), 0)
    across = lax.broadcasted_iota(jnp.int32, (TILE, 2 * LANES), 1)
    for member in range(rep_count):
        column = jnp.sum(jnp.where(across == tall + member * TILE, wide, 0.0), axis=1, keepdims=True)
        table_ref[member, :TILE] = jnp.broadcast_to(column, (TILE, LANES))
        table_ref[member, TILE:] = jnp.zeros((rows - TILE, LANES), jnp.float32)

    lane = lax.broadcasted_iota(jnp.int32, (rows, LANES), 1)
    spare = LANES - 8
    for plan, out_ref in zip(rounds(groups), out_refs):
        group = goes_to(plan, my_grp, my_rep)
        tile = group * rep_count + (my_rep ^ plan[2])
        chosen = [tile]
        member, place_of = jnp.int32(0), jnp.int32(-1)
        for slot in range(listed):
            other = pairs_ref[slot, tile]
            chosen.append(jnp.maximum(other, 0))
            among = other - my_grp * rep_count
            inside = (among >= 0) & (among < rep_count)
            member = jnp.where(inside, among, member)
            place_of = jnp.where(inside, slot + 1, place_of)
        own_at = jnp.where(group == my_grp, spare, -1)
        theirs = table_ref[member]
        mine = table_ref[my_rep]
        for block in range(packed // LANES):
            total = jnp.zeros((rows, LANES), jnp.float32)
            for place in range(PER_BLOCK):
                index = block * PER_BLOCK + place
                if index > listed:
                    continue
                start = chosen[index] * TILE
                source = start >> 7
                offset = start & (LANES - 1)
                both = jnp.where(lane >= offset, blocks_ref[source], blocks_ref[source + 1])
                shift = (place * TILE - offset) & (LANES - 1)
                moved = pltpu.roll(both, shift, 1)
                here = (lane >= place * TILE) & (lane < (place + 1) * TILE)
                total = jnp.where(here, moved, total)
            first = block * PER_BLOCK
            here = (place_of >= first) & (place_of < first + PER_BLOCK)
            marked = jnp.where(here, spare + place_of - first, -1)
            total = jnp.where(lane == marked, theirs, total)
            if block == 0:
                total = jnp.where(lane == own_at, mine, total)
            out_ref[:, block * LANES : (block + 1) * LANES] = total.astype(jnp.bfloat16)


def pack(strain, fir_taps, half_widths, pairs, groups, rep_count):
    channels, filled = strain.shape
    rows = max(filled, -(-TILE // 16) * 16)
    tiles, listed = pairs.shape
    members = half_widths.shape[0]
    packed = -(-(listed + 1) // PER_BLOCK) * LANES
    hbm = pl.BlockSpec(memory_space=pltpu.HBM)
    vmem = pl.BlockSpec(memory_space=pltpu.VMEM)
    return pl.pallas_call(
        functools.partial(pack_kernel, rep_count),
        out_shape=[jax.ShapeDtypeStruct((rows, packed), jnp.bfloat16)] * groups
        + [jax.ShapeDtypeStruct((1, fir_taps.shape[0]), jnp.float32)],
        in_specs=[hbm] * 4,
        out_specs=[vmem] * (groups + 1),
        scratch_shapes=[
            pltpu.SMEM((listed, tiles), jnp.int32),
            pltpu.VMEM((filled, channels), jnp.bfloat16),
            pltpu.VMEM((1, members), jnp.int32),
            pltpu.SemaphoreType.DMA((4,)),
            pltpu.VMEM((channels // LANES + 1, rows, LANES), jnp.float32),
            pltpu.VMEM((rep_count, rows, LANES), jnp.float32),
        ],
        compiler_params=pltpu.CompilerParams(vmem_limit_bytes=48 * 2**20),
        name="pack",
    )(*[
        pltpu.with_memory_space_constraint(array, pltpu.HBM)
        for array in (pairs.T, strain.T, half_widths[None, :], fir_taps[None, :])
    ])


def split(values):
    high = values.astype(jnp.bfloat16)
    low = (values - high.astype(jnp.float32)).astype(jnp.bfloat16)
    return high, low


def dot(left, right):
    return jnp.dot(left, right, preferred_element_type=jnp.float32)


def condition(period, raw_ref, taps_ref, white_ref):
    groups, rows, packed = raw_ref.shape
    listed = white_ref.shape[0] // TILE - 1
    blocks = packed // LANES
    raw = raw_ref[:, :period, :].astype(jnp.float32).reshape(groups * period, packed)
    samples = jnp.transpose(raw).astype(jnp.bfloat16)
    columns = []
    for block in range(blocks):
        piece = raw_ref[:, :TILE, block * LANES : (block + 1) * LANES].astype(jnp.float32)
        columns.append(jnp.sum(piece, axis=0))

    count = taps_ref.shape[1]
    taps = jnp.concatenate([taps_ref[...], jnp.zeros((1, 2 * LANES - count), jnp.float32)], axis=1)
    bands = pltpu.roll(jnp.broadcast_to(taps, (LANES, 2 * LANES)), 0, 1, stride=1, stride_axis=0)
    parts = []
    empty = jnp.zeros((LANES, LANES), jnp.bfloat16)
    for piece in split(bands):
        near, far = piece[:, :LANES], piece[:, LANES:]
        first = jnp.concatenate([piece, jnp.concatenate([empty, near], axis=1)], axis=0)
        second = jnp.concatenate([far, near], axis=0)
        parts.append((dot(samples[:, : 2 * LANES], first), dot(samples[:, LANES:], second)))
    filtered = jnp.concatenate([parts[0][0] + parts[1][0], parts[0][1] + parts[1][1]], axis=1)

    size = jnp.abs(filtered)
    before = lax.broadcasted_iota(jnp.int32, (2 * LANES, 2 * LANES), 0) <= lax.broadcasted_iota(
        jnp.int32, (2 * LANES, 2 * LANES), 1
    )
    upper = jnp.where(before, 1.0, 0.0).astype(jnp.bfloat16)
    ones = jnp.ones((2 * LANES, LANES), jnp.bfloat16)
    sums = []
    for piece in split(size):
        head, tail = piece[:, : 2 * LANES], piece[:, 2 * LANES :]
        sums.append((dot(head, upper), dot(head, ones), dot(tail, upper[:LANES, :LANES])))
    high, low = sums
    head = high[0] + low[0]
    tail = (high[1] + low[1]) + (high[2] + low[2])
    prefix = [head[:, :LANES], head[:, LANES:], tail]

    lane = lax.broadcasted_iota(jnp.int32, (TILE, LANES), 1)
    for slot in range(listed + 1):
        base = slot // PER_BLOCK * LANES + slot % PER_BLOCK * TILE
        at = slice(base, base + TILE)
        from_lane = LANES - 8 + slot % PER_BLOCK
        column = columns[slot // PER_BLOCK][:, from_lane : from_lane + 1]
        width = jnp.broadcast_to(column, (TILE, LANES))
        whole = width.astype(jnp.int32)
        above = lane + whole
        below = lane - whole - 1
        above_at = above & (LANES - 1)
        below_at = below & (LANES - 1)
        above_by = above >> 7
        below_by = below >> 7
        up = [jnp.take_along_axis(prefix[b][at], above_at, axis=1) for b in range(3)]
        down = [jnp.take_along_axis(prefix[b][at], below_at, axis=1) for b in range(2)]
        full = jnp.broadcast_to(prefix[2][at][:, LANES - 1 :], (TILE, LANES))
        ends = up + [full, full]
        starts = [jnp.zeros((TILE, LANES), jnp.float32)] * 2 + down
        down_last = jnp.take_along_axis(prefix[2][at], below_at, axis=1)
        starts.append(down_last)
        scale = 1.0 / (2.0 * width + 1.0)
        high_0, high_1 = above_by == 0, above_by == 1
        low_0, low_1 = below_by == 0, below_by == -1
        for block in range(3 if slot else 1):
            top = jnp.where(high_0, ends[block], jnp.where(high_1, ends[block + 1], ends[block + 2]))
            low_end = jnp.where(
                low_0, starts[block + 2], jnp.where(low_1, starts[block + 1], starts[block])
            )
            level = (top - low_end) * scale
            value = filtered[at, block * LANES : (block + 1) * LANES] / (level + 1e-05)
            if slot:
                value = jnp.where(width > 0.0, value, 0.0)
            white_ref[slot * TILE : (slot + 1) * TILE, block * LANES : (block + 1) * LANES] = value


def correlate_kernel(period, taps_ref, *refs):
    received = refs[:-11]
    out_hbm, raw_ref, white_ref, partner_ref, reverse_ref = refs[-11:-6]
    low_even, high_even, low_odd, high_odd, packed_ref, semaphores = refs[-6:]
    groups = len(received)
    my_grp = lax.axis_index("grp")
    my_rep = lax.axis_index("rep")
    for plan, ref in zip(rounds(groups), received):
        raw_ref[comes_from(plan, my_grp, my_rep)] = ref[...]
    condition(period, raw_ref, taps_ref, white_ref)

    own = white_ref[:TILE, :LANES].astype(jnp.bfloat16)
    row = lax.broadcasted_iota(jnp.int32, (LANES, LANES), 0)
    col = lax.broadcasted_iota(jnp.int32, (LANES, LANES), 1)
    flip = jnp.where(row + col == LANES - 1, 1.0, 0.0).astype(jnp.bfloat16)
    reverse_ref[...] = dot(own, flip)
    partner = white_ref[TILE:, :].astype(jnp.bfloat16)
    rows = partner.shape[0]
    partner_ref[:rows] = partner[:, : 2 * LANES]
    partner_ref[rows:] = partner[:, LANES:]
    listed = rows // TILE
    normalizer = 1.0 / math.sqrt(LANES)
    keep = col <= row
    even, odd = (low_even, high_even), (low_odd, high_odd)
    count = TILE // 8
    parts = 4
    share = listed // parts

    def band(channel):
        line = jnp.broadcast_to(reverse_ref[pl.ds(channel, 1), :], (LANES, LANES))
        turned = pltpu.roll(line, 1, 1, stride=1, stride_axis=0)
        first = jnp.where(keep, turned, 0.0).astype(jnp.bfloat16)
        second = jnp.where(keep, 0.0, turned).astype(jnp.bfloat16)
        return jnp.concatenate([first, second], axis=0)

    def outgoing(group, part):
        tiles = pl.ds(part * share, share)
        return pltpu.make_async_copy(
            packed_ref.at[group, tiles],
            out_hbm.at[0, tiles, :, pl.ds(group * 8, 8), :],
            semaphores.at[group, part],
        )

    wide = 4

    def multiply(group, part, held):
        channel = group * 8 + wide * part
        weights = jnp.concatenate([band(channel + side) for side in range(wide)], axis=1)
        product = dot(partner_ref[...], weights) * normalizer
        for half, ref in enumerate(held):
            for side in range(wide):
                ref[pl.ds(wide * part + side, rows, stride=STRIDE), :] = product[
                    half * rows : (half + 1) * rows, side * LANES : (side + 1) * LANES
                ]

    def convert(group, part, held):
        for tile in range(part * share, (part + 1) * share):
            for line in range(TILE):
                at = pl.ds((tile * TILE + line) * STRIDE, 8)
                both = jnp.concatenate([ref[at, :] for ref in held], axis=1)
                packed_ref[group, tile, line] = both.astype(jnp.bfloat16)

    def together(group, held, before):
        for part in range(parts):
            if part % 2 == 0:
                multiply(group, part // 2, held)
            convert(group - 1, part, before)
            if part % 2:
                outgoing(group - 1, part - 1).start(priority=0)
                outgoing(group - 1, part).start(priority=1)

    for part in range(8 // wide):
        multiply(0, part, even)

    def two_groups(index, carry):
        together(2 * index + 1, odd, even)
        together(2 * index + 2, even, odd)
        return carry

    lax.fori_loop(0, count // 2, two_groups, 0)
    for part in range(parts):
        convert(count - 1, part, even)
        outgoing(count - 1, part).start(priority=part % 2)
    for group in range(count):
        for part in range(parts):
            outgoing(group, part).wait()


def correlate(received, taps, period, listed):
    groups = len(received)
    rows, packed = received[0].shape
    lines = listed * TILE
    vmem = pl.BlockSpec(memory_space=pltpu.VMEM)
    return pl.pallas_call(
        functools.partial(correlate_kernel, period),
        out_shape=jax.ShapeDtypeStruct((1, listed, TILE, TILE, LAGS), jnp.bfloat16),
        in_specs=[vmem] * (groups + 1),
        out_specs=pl.BlockSpec(memory_space=pltpu.HBM),
        scratch_shapes=[
            pltpu.VMEM((groups, rows, packed), jnp.bfloat16),
            pltpu.VMEM(((listed + 1) * TILE, groups * period), jnp.float32),
            pltpu.VMEM((2 * lines, 2 * LANES), jnp.bfloat16),
            pltpu.VMEM((TILE, LANES), jnp.float32),
        ]
        + [pltpu.VMEM((lines * STRIDE, LANES), jnp.float32)] * 4
        + [
            pltpu.VMEM((TILE // 8, listed, TILE, 8, LAGS), jnp.bfloat16),
            pltpu.SemaphoreType.DMA((TILE // 8, 4)),
        ],
        compiler_params=pltpu.CompilerParams(vmem_limit_bytes=40 * 2**20),
        name="correlate",
    )(taps, *received)


def on_device(strain, fir_taps, half_widths, pairs):
    groups = lax.axis_size("grp")
    rep_count = lax.axis_size("rep")
    *messages, taps = pack(strain, fir_taps, half_widths, pairs, groups, rep_count)
    received = []
    for plan, message in zip(rounds(groups), messages):
        if plan[0] != tuple(range(groups)):
            way = [
                (group * rep_count + member, plan[member % 2][group] * rep_count + (member ^ plan[2]))
                for group in range(groups)
                for member in range(rep_count)
            ]
            message = lax.ppermute(message, ("grp", "rep"), way)
        received.append(message)
    return correlate(received, taps, strain.shape[1], pairs.shape[1])


def solution(mesh):
    placed = (P(None, "grp"), P(), P("grp"), P())
    return jax.shard_map(
        on_device,
        mesh=mesh,
        in_specs=placed,
        out_specs=P(("grp", "rep"), None, None, None, None),
        check_vma=False,
    )
```

```python
import functools
import math

import jax
import jax.numpy as jnp
from jax import lax
from jax.experimental import pallas as pl
from jax.experimental.pallas import tpu as pltpu
from jax.sharding import PartitionSpec as P

TILE = 40
LAGS = 256
LANES = 128
STRIDE = 9
PER_BLOCK = LANES // TILE


def fetch(pairs, semaphores):
    copies = [
        pltpu.make_async_copy(source, target, semaphores.at[index])
        for index, (source, target) in enumerate(pairs)
    ]
    for copy in copies:
        copy.start()
    for copy in copies:
        copy.wait()


ROUTES = (
    ((2, 3, 4, 5, 6, 7, 0, 1), (3, 2, 5, 4, 7, 6, 1, 0), 0),
    ((2, 3, 4, 5, 6, 7, 0, 1), (5, 4, 7, 6, 1, 0, 3, 2), 1),
    ((1, 0, 3, 2, 5, 4, 7, 6), (7, 6, 1, 0, 3, 2, 5, 4), 1),
    ((4, 5, 6, 7, 0, 1, 2, 3), (7, 6, 1, 0, 3, 2, 5, 4), 0),
    ((4, 5, 6, 7, 0, 1, 2, 3), (3, 2, 5, 4, 7, 6, 1, 0), 1),
    ((1, 0, 3, 2, 5, 4, 7, 6), (5, 4, 7, 6, 1, 0, 3, 2), 0),
    ((6, 7, 0, 1, 2, 3, 4, 5), (6, 7, 0, 1, 2, 3, 4, 5), 0),
)


def rounds(groups):
    stay = tuple(range(groups))
    if groups == len(ROUTES[0][0]):
        return list(ROUTES) + [(stay, stay, 0)]
    steps = [tuple(group ^ step for group in range(groups)) for step in reversed(range(groups))]
    return [(route, route, 0) for route in steps]


def goes_to(plan, group, member):
    even, odd, _ = plan
    if even == odd:
        return pick(even, group)
    return jnp.where(lax.rem(member, 2) == 0, pick(even, group), pick(odd, group))


def comes_from(plan, group, member):
    even, odd, crossed = plan
    return goes_to((inverse(even), inverse(odd), 0), group, member ^ crossed)


def inverse(route):
    return tuple(route.index(group) for group in range(len(route)))


def pick(route, group):
    if len(route) > 8:
        return group ^ route[0]
    code = sum(target << (3 * index) for index, target in enumerate(route))
    return (jnp.int32(code) >> (3 * group)) & 7


def pack_kernel(rep_count, pairs_hbm, strain_hbm, widths_hbm, taps_hbm, *refs):
    out_refs = refs[:-7]
    taps_ref = refs[-7]
    pairs_ref, strain_ref, widths_ref, semaphores, blocks_ref, table_ref = refs[-6:]
    groups = len(out_refs)
    rows, packed = out_refs[0].shape
    listed = pairs_ref.shape[0]
    channels = strain_ref.shape[1]
    members = widths_ref.shape[1]
    fetch(
        [
            (strain_hbm, strain_ref),
            (pairs_hbm, pairs_ref),
            (widths_hbm, widths_ref),
            (taps_hbm, taps_ref),
        ],
        semaphores,
    )
    my_rep = lax.axis_index("rep")
    my_grp = lax.axis_index("grp")

    count = channels // LANES
    filled = strain_ref.shape[0]
    for block in range(count):
        values = strain_ref[:, block * LANES : (block + 1) * LANES].astype(jnp.float32)
        if rows > filled:
            values = jnp.concatenate([values, jnp.zeros((rows - filled, LANES), jnp.float32)], axis=0)
        blocks_ref[block] = values
    blocks_ref[count] = jnp.zeros((rows, LANES), jnp.float32)

    wide = jnp.concatenate(
        [widths_ref[...].astype(jnp.float32), jnp.zeros((1, 2 * LANES - members), jnp.float32)],
        axis=1,
    )
    wide = jnp.broadcast_to(wide, (TILE, 2 * LANES))
    tall = lax.broadcasted_iota(jnp.int32, (TILE, 2 * LANES), 0)
    across = lax.broadcasted_iota(jnp.int32, (TILE, 2 * LANES), 1)
    for member in range(rep_count):
        column = jnp.sum(jnp.where(across == tall + member * TILE, wide, 0.0), axis=1, keepdims=True)
        table_ref[member, :TILE] = jnp.broadcast_to(column, (TILE, LANES))
        table_ref[member, TILE:] = jnp.zeros((rows - TILE, LANES), jnp.float32)

    lane = lax.broadcasted_iota(jnp.int32, (rows, LANES), 1)
    spare = LANES - 8
    for plan, out_ref in zip(rounds(groups), out_refs):
        group = goes_to(plan, my_grp, my_rep)
        tile = group * rep_count + (my_rep ^ plan[2])
        chosen = [tile]
        member, place_of = jnp.int32(0), jnp.int32(-1)
        for slot in range(listed):
            other = pairs_ref[slot, tile]
            chosen.append(jnp.maximum(other, 0))
            among = other - my_grp * rep_count
            inside = (among >= 0) & (among < rep_count)
            member = jnp.where(inside, among, member)
            place_of = jnp.where(inside, slot + 1, place_of)
        own_at = jnp.where(group == my_grp, spare, -1)
        theirs = table_ref[member]
        mine = table_ref[my_rep]
        for block in range(packed // LANES):
            total = jnp.zeros((rows, LANES), jnp.float32)
            for place in range(PER_BLOCK):
                index = block * PER_BLOCK + place
                if index > listed:
                    continue
                start = chosen[index] * TILE
                source = start >> 7
                offset = start & (LANES - 1)
                both = jnp.where(lane >= offset, blocks_ref[source], blocks_ref[source + 1])
                shift = (place * TILE - offset) & (LANES - 1)
                moved = pltpu.roll(both, shift, 1)
                here = (lane >= place * TILE) & (lane < (place + 1) * TILE)
                total = jnp.where(here, moved, total)
            first = block * PER_BLOCK
            here = (place_of >= first) & (place_of < first + PER_BLOCK)
            marked = jnp.where(here, spare + place_of - first, -1)
            total = jnp.where(lane == marked, theirs, total)
            if block == 0:
                total = jnp.where(lane == own_at, mine, total)
            out_ref[:, block * LANES : (block + 1) * LANES] = total.astype(jnp.bfloat16)


def pack(strain, fir_taps, half_widths, pairs, groups, rep_count):
    channels, filled = strain.shape
    rows = max(filled, -(-TILE // 16) * 16)
    tiles, listed = pairs.shape
    members = half_widths.shape[0]
    packed = -(-(listed + 1) // PER_BLOCK) * LANES
    hbm = pl.BlockSpec(memory_space=pltpu.HBM)
    vmem = pl.BlockSpec(memory_space=pltpu.VMEM)
    return pl.pallas_call(
        functools.partial(pack_kernel, rep_count),
        out_shape=[jax.ShapeDtypeStruct((rows, packed), jnp.bfloat16)] * groups
        + [jax.ShapeDtypeStruct((1, fir_taps.shape[0]), jnp.float32)],
        in_specs=[hbm] * 4,
        out_specs=[vmem] * (groups + 1),
        scratch_shapes=[
            pltpu.SMEM((listed, tiles), jnp.int32),
            pltpu.VMEM((filled, channels), jnp.bfloat16),
            pltpu.VMEM((1, members), jnp.int32),
            pltpu.SemaphoreType.DMA((4,)),
            pltpu.VMEM((channels // LANES + 1, rows, LANES), jnp.float32),
            pltpu.VMEM((rep_count, rows, LANES), jnp.float32),
        ],
        compiler_params=pltpu.CompilerParams(vmem_limit_bytes=48 * 2**20),
        name="pack",
    )(*[
        pltpu.with_memory_space_constraint(array, pltpu.HBM)
        for array in (pairs.T, strain.T, half_widths[None, :], fir_taps[None, :])
    ])


def split(values):
    high = values.astype(jnp.bfloat16)
    low = (values - high.astype(jnp.float32)).astype(jnp.bfloat16)
    return high, low


def dot(left, right):
    return jnp.dot(left, right, preferred_element_type=jnp.float32)


def condition(period, raw_ref, taps_ref, white_ref):
    groups, rows, packed = raw_ref.shape
    listed = white_ref.shape[0] // TILE - 1
    blocks = packed // LANES
    raw = raw_ref[:, :period, :].astype(jnp.float32).reshape(groups * period, packed)
    samples = jnp.transpose(raw).astype(jnp.bfloat16)
    columns = []
    for block in range(blocks):
        piece = raw_ref[:, :TILE, block * LANES : (block + 1) * LANES].astype(jnp.float32)
        columns.append(jnp.sum(piece, axis=0))

    count = taps_ref.shape[1]
    taps = jnp.concatenate([taps_ref[...], jnp.zeros((1, 2 * LANES - count), jnp.float32)], axis=1)
    bands = pltpu.roll(jnp.broadcast_to(taps, (LANES, 2 * LANES)), 0, 1, stride=1, stride_axis=0)
    parts = []
    empty = jnp.zeros((LANES, LANES), jnp.bfloat16)
    for piece in split(bands):
        near, far = piece[:, :LANES], piece[:, LANES:]
        first = jnp.concatenate([piece, jnp.concatenate([empty, near], axis=1)], axis=0)
        second = jnp.concatenate([far, near], axis=0)
        parts.append((dot(samples[:, : 2 * LANES], first), dot(samples[:, LANES:], second)))
    filtered = jnp.concatenate([parts[0][0] + parts[1][0], parts[0][1] + parts[1][1]], axis=1)

    size = jnp.abs(filtered)
    before = lax.broadcasted_iota(jnp.int32, (2 * LANES, 2 * LANES), 0) <= lax.broadcasted_iota(
        jnp.int32, (2 * LANES, 2 * LANES), 1
    )
    upper = jnp.where(before, 1.0, 0.0).astype(jnp.bfloat16)
    ones = jnp.ones((2 * LANES, LANES), jnp.bfloat16)
    sums = []
    for piece in split(size):
        head, tail = piece[:, : 2 * LANES], piece[:, 2 * LANES :]
        sums.append((dot(head, upper), dot(head, ones), dot(tail, upper[:LANES, :LANES])))
    high, low = sums
    head = high[0] + low[0]
    tail = (high[1] + low[1]) + (high[2] + low[2])
    prefix = [head[:, :LANES], head[:, LANES:], tail]

    lane = lax.broadcasted_iota(jnp.int32, (TILE, LANES), 1)
    for slot in range(listed + 1):
        base = slot // PER_BLOCK * LANES + slot % PER_BLOCK * TILE
        at = slice(base, base + TILE)
        from_lane = LANES - 8 + slot % PER_BLOCK
        column = columns[slot // PER_BLOCK][:, from_lane : from_lane + 1]
        width = jnp.broadcast_to(column, (TILE, LANES))
        whole = width.astype(jnp.int32)
        above = lane + whole
        below = lane - whole - 1
        above_at = above & (LANES - 1)
        below_at = below & (LANES - 1)
        above_by = above >> 7
        below_by = below >> 7
        up = [jnp.take_along_axis(prefix[b][at], above_at, axis=1) for b in range(3)]
        down = [jnp.take_along_axis(prefix[b][at], below_at, axis=1) for b in range(2)]
        full = jnp.broadcast_to(prefix[2][at][:, LANES - 1 :], (TILE, LANES))
        ends = up + [full, full]
        starts = [jnp.zeros((TILE, LANES), jnp.float32)] * 2 + down
        down_last = jnp.take_along_axis(prefix[2][at], below_at, axis=1)
        starts.append(down_last)
        scale = 1.0 / (2.0 * width + 1.0)
        high_0, high_1 = above_by == 0, above_by == 1
        low_0, low_1 = below_by == 0, below_by == -1
        for block in range(3 if slot else 1):
            top = jnp.where(high_0, ends[block], jnp.where(high_1, ends[block + 1], ends[block + 2]))
            low_end = jnp.where(
                low_0, starts[block + 2], jnp.where(low_1, starts[block + 1], starts[block])
            )
            level = (top - low_end) * scale
            value = filtered[at, block * LANES : (block + 1) * LANES] / (level + 1e-05)
            if slot:
                value = jnp.where(width > 0.0, value, 0.0)
            white_ref[slot * TILE : (slot + 1) * TILE, block * LANES : (block + 1) * LANES] = value


def correlate_kernel(period, taps_ref, *refs):
    received = refs[:-11]
    out_hbm, raw_ref, white_ref, partner_ref, reverse_ref = refs[-11:-6]
    low_even, high_even, low_odd, high_odd, packed_ref, semaphores = refs[-6:]
    groups = len(received)
    my_grp = lax.axis_index("grp")
    my_rep = lax.axis_index("rep")
    for plan, ref in zip(rounds(groups), received):
        raw_ref[comes_from(plan, my_grp, my_rep)] = ref[...]
    condition(period, raw_ref, taps_ref, white_ref)

    own = white_ref[:TILE, :LANES].astype(jnp.bfloat16)
    row = lax.broadcasted_iota(jnp.int32, (LANES, LANES), 0)
    col = lax.broadcasted_iota(jnp.int32, (LANES, LANES), 1)
    flip = jnp.where(row + col == LANES - 1, 1.0, 0.0).astype(jnp.bfloat16)
    reverse_ref[...] = dot(own, flip)
    partner = white_ref[TILE:, :].astype(jnp.bfloat16)
    rows = partner.shape[0]
    partner_ref[:rows] = partner[:, : 2 * LANES]
    partner_ref[rows:] = partner[:, LANES:]
    listed = rows // TILE
    normalizer = 1.0 / math.sqrt(LANES)
    keep = col <= row
    even, odd = (low_even, high_even), (low_odd, high_odd)
    count = TILE // 8
    parts = 4
    share = listed // parts

    def band(channel):
        line = jnp.broadcast_to(reverse_ref[pl.ds(channel, 1), :], (LANES, LANES))
        turned = pltpu.roll(line, 1, 1, stride=1, stride_axis=0)
        first = jnp.where(keep, turned, 0.0).astype(jnp.bfloat16)
        second = jnp.where(keep, 0.0, turned).astype(jnp.bfloat16)
        return jnp.concatenate([first, second], axis=0)

    def outgoing(group, part):
        tiles = pl.ds(part * share, share)
        return pltpu.make_async_copy(
            packed_ref.at[group, tiles],
            out_hbm.at[0, tiles, :, pl.ds(group * 8, 8), :],
            semaphores.at[group, part],
        )

    wide = 4

    def multiply(group, part, held):
        channel = group * 8 + wide * part
        weights = jnp.concatenate([band(channel + side) for side in range(wide)], axis=1)
        product = dot(partner_ref[...], weights) * normalizer
        for half, ref in enumerate(held):
            for side in range(wide):
                ref[pl.ds(wide * part + side, rows, stride=STRIDE), :] = product[
                    half * rows : (half + 1) * rows, side * LANES : (side + 1) * LANES
                ]

    def convert(group, part, held):
        for tile in range(part * share, (part + 1) * share):
            for line in range(TILE):
                at = pl.ds((tile * TILE + line) * STRIDE, 8)
                both = jnp.concatenate([ref[at, :] for ref in held], axis=1)
                packed_ref[group, tile, line] = both.astype(jnp.bfloat16)

    def together(group, held, before):
        for part in range(parts):
            if part % 2 == 0:
                multiply(group, part // 2, held)
            convert(group - 1, part, before)
            outgoing(group - 1, part).start(priority=part % 2)

    for part in range(8 // wide):
        multiply(0, part, even)

    def two_groups(index, carry):
        together(2 * index + 1, odd, even)
        together(2 * index + 2, even, odd)
        return carry

    lax.fori_loop(0, count // 2, two_groups, 0)
    for part in range(parts):
        convert(count - 1, part, even)
        outgoing(count - 1, part).start(priority=part % 2)
    for group in range(count):
        for part in range(parts):
            outgoing(group, part).wait()


def correlate(received, taps, period, listed):
    groups = len(received)
    rows, packed = received[0].shape
    lines = listed * TILE
    vmem = pl.BlockSpec(memory_space=pltpu.VMEM)
    return pl.pallas_call(
        functools.partial(correlate_kernel, period),
        out_shape=jax.ShapeDtypeStruct((1, listed, TILE, TILE, LAGS), jnp.bfloat16),
        in_specs=[vmem] * (groups + 1),
        out_specs=pl.BlockSpec(memory_space=pltpu.HBM),
        scratch_shapes=[
            pltpu.VMEM((groups, rows, packed), jnp.bfloat16),
            pltpu.VMEM(((listed + 1) * TILE, groups * period), jnp.float32),
            pltpu.VMEM((2 * lines, 2 * LANES), jnp.bfloat16),
            pltpu.VMEM((TILE, LANES), jnp.float32),
        ]
        + [pltpu.VMEM((lines * STRIDE, LANES), jnp.float32)] * 4
        + [
            pltpu.VMEM((TILE // 8, listed, TILE, 8, LAGS), jnp.bfloat16),
            pltpu.SemaphoreType.DMA((TILE // 8, 4)),
        ],
        compiler_params=pltpu.CompilerParams(vmem_limit_bytes=40 * 2**20),
        name="correlate",
    )(taps, *received)


def on_device(strain, fir_taps, half_widths, pairs):
    groups = lax.axis_size("grp")
    rep_count = lax.axis_size("rep")
    *messages, taps = pack(strain, fir_taps, half_widths, pairs, groups, rep_count)
    received = []
    for plan, message in zip(rounds(groups), messages):
        if plan[0] != tuple(range(groups)):
            way = [
                (group * rep_count + member, plan[member % 2][group] * rep_count + (member ^ plan[2]))
                for group in range(groups)
                for member in range(rep_count)
            ]
            message = lax.ppermute(message, ("grp", "rep"), way)
        received.append(message)
    return correlate(received, taps, strain.shape[1], pairs.shape[1])


def solution(mesh):
    placed = (P(None, "grp"), P(), P("grp"), P())
    return jax.shard_map(
        on_device,
        mesh=mesh,
        in_specs=placed,
        out_specs=P(("grp", "rep"), None, None, None, None),
        check_vma=False,
    )
```

```python
import functools
import math

import jax
import jax.numpy as jnp
from jax import lax
from jax.experimental import pallas as pl
from jax.experimental.pallas import tpu as pltpu
from jax.sharding import PartitionSpec as P

TILE = 40
LAGS = 256
LANES = 128
STRIDE = 9
PER_BLOCK = LANES // TILE


def fetch(pairs, semaphores):
    copies = [
        pltpu.make_async_copy(source, target, semaphores.at[index])
        for index, (source, target) in enumerate(pairs)
    ]
    for copy in copies:
        copy.start()
    for copy in copies:
        copy.wait()


ROUTES = (
    ((2, 3, 4, 5, 6, 7, 0, 1), (3, 2, 5, 4, 7, 6, 1, 0), 0),
    ((2, 3, 4, 5, 6, 7, 0, 1), (5, 4, 7, 6, 1, 0, 3, 2), 1),
    ((1, 0, 3, 2, 5, 4, 7, 6), (7, 6, 1, 0, 3, 2, 5, 4), 1),
    ((4, 5, 6, 7, 0, 1, 2, 3), (7, 6, 1, 0, 3, 2, 5, 4), 0),
    ((4, 5, 6, 7, 0, 1, 2, 3), (3, 2, 5, 4, 7, 6, 1, 0), 1),
    ((1, 0, 3, 2, 5, 4, 7, 6), (5, 4, 7, 6, 1, 0, 3, 2), 0),
    ((6, 7, 0, 1, 2, 3, 4, 5), (6, 7, 0, 1, 2, 3, 4, 5), 0),
)


def rounds(groups):
    stay = tuple(range(groups))
    if groups == len(ROUTES[0][0]):
        return list(ROUTES) + [(stay, stay, 0)]
    steps = [tuple(group ^ step for group in range(groups)) for step in reversed(range(groups))]
    return [(route, route, 0) for route in steps]


def goes_to(plan, group, member):
    even, odd, _ = plan
    if even == odd:
        return pick(even, group)
    return jnp.where(lax.rem(member, 2) == 0, pick(even, group), pick(odd, group))


def comes_from(plan, group, member):
    even, odd, crossed = plan
    return goes_to((inverse(even), inverse(odd), 0), group, member ^ crossed)


def inverse(route):
    return tuple(route.index(group) for group in range(len(route)))


def pick(route, group):
    if len(route) > 8:
        return group ^ route[0]
    code = sum(target << (3 * index) for index, target in enumerate(route))
    return (jnp.int32(code) >> (3 * group)) & 7


def pack_kernel(rep_count, pairs_hbm, strain_hbm, widths_hbm, taps_hbm, *refs):
    out_refs = refs[:-7]
    taps_ref = refs[-7]
    pairs_ref, strain_ref, widths_ref, semaphores, blocks_ref, table_ref = refs[-6:]
    groups = len(out_refs)
    rows, packed = out_refs[0].shape
    listed = pairs_ref.shape[0]
    channels = strain_ref.shape[1]
    members = widths_ref.shape[1]
    fetch(
        [
            (strain_hbm, strain_ref),
            (pairs_hbm, pairs_ref),
            (widths_hbm, widths_ref),
            (taps_hbm, taps_ref),
        ],
        semaphores,
    )
    my_rep = lax.axis_index("rep")
    my_grp = lax.axis_index("grp")

    count = channels // LANES
    filled = strain_ref.shape[0]
    for block in range(count):
        values = strain_ref[:, block * LANES : (block + 1) * LANES].astype(jnp.float32)
        if rows > filled:
            values = jnp.concatenate([values, jnp.zeros((rows - filled, LANES), jnp.float32)], axis=0)
        blocks_ref[block] = values
    blocks_ref[count] = jnp.zeros((rows, LANES), jnp.float32)

    wide = jnp.concatenate(
        [widths_ref[...].astype(jnp.float32), jnp.zeros((1, 2 * LANES - members), jnp.float32)],
        axis=1,
    )
    wide = jnp.broadcast_to(wide, (TILE, 2 * LANES))
    tall = lax.broadcasted_iota(jnp.int32, (TILE, 2 * LANES), 0)
    across = lax.broadcasted_iota(jnp.int32, (TILE, 2 * LANES), 1)
    for member in range(rep_count):
        column = jnp.sum(jnp.where(across == tall + member * TILE, wide, 0.0), axis=1, keepdims=True)
        table_ref[member, :TILE] = jnp.broadcast_to(column, (TILE, LANES))
        table_ref[member, TILE:] = jnp.zeros((rows - TILE, LANES), jnp.float32)

    lane = lax.broadcasted_iota(jnp.int32, (rows, LANES), 1)
    spare = LANES - 8
    for plan, out_ref in zip(rounds(groups), out_refs):
        group = goes_to(plan, my_grp, my_rep)
        tile = group * rep_count + (my_rep ^ plan[2])
        chosen = [tile]
        member, place_of = jnp.int32(0), jnp.int32(-1)
        for slot in range(listed):
            other = pairs_ref[slot, tile]
            chosen.append(jnp.maximum(other, 0))
            among = other - my_grp * rep_count
            inside = (among >= 0) & (among < rep_count)
            member = jnp.where(inside, among, member)
            place_of = jnp.where(inside, slot + 1, place_of)
        own_at = jnp.where(group == my_grp, spare, -1)
        theirs = table_ref[member]
        mine = table_ref[my_rep]
        for block in range(packed // LANES):
            total = jnp.zeros((rows, LANES), jnp.float32)
            for place in range(PER_BLOCK):
                index = block * PER_BLOCK + place
                if index > listed:
                    continue
                start = chosen[index] * TILE
                source = start >> 7
                offset = start & (LANES - 1)
                both = jnp.where(lane >= offset, blocks_ref[source], blocks_ref[source + 1])
                shift = (place * TILE - offset) & (LANES - 1)
                moved = pltpu.roll(both, shift, 1)
                here = (lane >= place * TILE) & (lane < (place + 1) * TILE)
                total = jnp.where(here, moved, total)
            first = block * PER_BLOCK
            here = (place_of >= first) & (place_of < first + PER_BLOCK)
            marked = jnp.where(here, spare + place_of - first, -1)
            total = jnp.where(lane == marked, theirs, total)
            if block == 0:
                total = jnp.where(lane == own_at, mine, total)
            out_ref[:, block * LANES : (block + 1) * LANES] = total.astype(jnp.bfloat16)


def pack(strain, fir_taps, half_widths, pairs, groups, rep_count):
    channels, filled = strain.shape
    rows = max(filled, -(-TILE // 16) * 16)
    tiles, listed = pairs.shape
    members = half_widths.shape[0]
    packed = -(-(listed + 1) // PER_BLOCK) * LANES
    hbm = pl.BlockSpec(memory_space=pltpu.HBM)
    vmem = pl.BlockSpec(memory_space=pltpu.VMEM)
    return pl.pallas_call(
        functools.partial(pack_kernel, rep_count),
        out_shape=[jax.ShapeDtypeStruct((rows, packed), jnp.bfloat16)] * groups
        + [jax.ShapeDtypeStruct((1, fir_taps.shape[0]), jnp.float32)],
        in_specs=[hbm] * 4,
        out_specs=[vmem] * (groups + 1),
        scratch_shapes=[
            pltpu.SMEM((listed, tiles), jnp.int32),
            pltpu.VMEM((filled, channels), jnp.bfloat16),
            pltpu.VMEM((1, members), jnp.int32),
            pltpu.SemaphoreType.DMA((4,)),
            pltpu.VMEM((channels // LANES + 1, rows, LANES), jnp.float32),
            pltpu.VMEM((rep_count, rows, LANES), jnp.float32),
        ],
        compiler_params=pltpu.CompilerParams(vmem_limit_bytes=48 * 2**20),
        name="pack",
    )(*[
        pltpu.with_memory_space_constraint(array, pltpu.HBM)
        for array in (pairs.T, strain.T, half_widths[None, :], fir_taps[None, :])
    ])


def split(values):
    high = values.astype(jnp.bfloat16)
    low = (values - high.astype(jnp.float32)).astype(jnp.bfloat16)
    return high, low


def dot(left, right):
    return jnp.dot(left, right, preferred_element_type=jnp.float32)


def condition(period, raw_ref, taps_ref, white_ref):
    groups, rows, packed = raw_ref.shape
    listed = white_ref.shape[0] // TILE - 1
    blocks = packed // LANES
    raw = raw_ref[:, :period, :].astype(jnp.float32).reshape(groups * period, packed)
    samples = jnp.transpose(raw).astype(jnp.bfloat16)
    columns = []
    for block in range(blocks):
        piece = raw_ref[:, :TILE, block * LANES : (block + 1) * LANES].astype(jnp.float32)
        columns.append(jnp.sum(piece, axis=0))

    count = taps_ref.shape[1]
    taps = jnp.concatenate([taps_ref[...], jnp.zeros((1, 2 * LANES - count), jnp.float32)], axis=1)
    bands = pltpu.roll(jnp.broadcast_to(taps, (LANES, 2 * LANES)), 0, 1, stride=1, stride_axis=0)
    parts = []
    empty = jnp.zeros((LANES, LANES), jnp.bfloat16)
    for piece in split(bands):
        near, far = piece[:, :LANES], piece[:, LANES:]
        first = jnp.concatenate([piece, jnp.concatenate([empty, near], axis=1)], axis=0)
        second = jnp.concatenate([far, near], axis=0)
        parts.append((dot(samples[:, : 2 * LANES], first), dot(samples[:, LANES:], second)))
    filtered = jnp.concatenate([parts[0][0] + parts[1][0], parts[0][1] + parts[1][1]], axis=1)

    size = jnp.abs(filtered)
    before = lax.broadcasted_iota(jnp.int32, (2 * LANES, 2 * LANES), 0) <= lax.broadcasted_iota(
        jnp.int32, (2 * LANES, 2 * LANES), 1
    )
    upper = jnp.where(before, 1.0, 0.0).astype(jnp.bfloat16)
    ones = jnp.ones((2 * LANES, LANES), jnp.bfloat16)
    sums = []
    for piece in split(size):
        head, tail = piece[:, : 2 * LANES], piece[:, 2 * LANES :]
        sums.append((dot(head, upper), dot(head, ones), dot(tail, upper[:LANES, :LANES])))
    high, low = sums
    head = high[0] + low[0]
    tail = (high[1] + low[1]) + (high[2] + low[2])
    prefix = [head[:, :LANES], head[:, LANES:], tail]

    lane = lax.broadcasted_iota(jnp.int32, (TILE, LANES), 1)
    for slot in range(listed + 1):
        base = slot // PER_BLOCK * LANES + slot % PER_BLOCK * TILE
        at = slice(base, base + TILE)
        from_lane = LANES - 8 + slot % PER_BLOCK
        column = columns[slot // PER_BLOCK][:, from_lane : from_lane + 1]
        width = jnp.broadcast_to(column, (TILE, LANES))
        whole = width.astype(jnp.int32)
        above = lane + whole
        below = lane - whole - 1
        above_at = above & (LANES - 1)
        below_at = below & (LANES - 1)
        above_by = above >> 7
        below_by = below >> 7
        up = [jnp.take_along_axis(prefix[b][at], above_at, axis=1) for b in range(3)]
        down = [jnp.take_along_axis(prefix[b][at], below_at, axis=1) for b in range(2)]
        full = jnp.broadcast_to(prefix[2][at][:, LANES - 1 :], (TILE, LANES))
        ends = up + [full, full]
        starts = [jnp.zeros((TILE, LANES), jnp.float32)] * 2 + down
        down_last = jnp.take_along_axis(prefix[2][at], below_at, axis=1)
        starts.append(down_last)
        scale = 1.0 / (2.0 * width + 1.0)
        high_0, high_1 = above_by == 0, above_by == 1
        low_0, low_1 = below_by == 0, below_by == -1
        for block in range(3 if slot else 1):
            top = jnp.where(high_0, ends[block], jnp.where(high_1, ends[block + 1], ends[block + 2]))
            low_end = jnp.where(
                low_0, starts[block + 2], jnp.where(low_1, starts[block + 1], starts[block])
            )
            level = (top - low_end) * scale
            value = filtered[at, block * LANES : (block + 1) * LANES] / (level + 1e-05)
            if slot:
                value = jnp.where(width > 0.0, value, 0.0)
            white_ref[slot * TILE : (slot + 1) * TILE, block * LANES : (block + 1) * LANES] = value


def correlate_kernel(period, taps_ref, *refs):
    received = refs[:-11]
    out_hbm, raw_ref, white_ref, partner_ref, reverse_ref = refs[-11:-6]
    low_even, high_even, low_odd, high_odd, packed_ref, semaphores = refs[-6:]
    groups = len(received)
    my_grp = lax.axis_index("grp")
    my_rep = lax.axis_index("rep")
    for plan, ref in zip(rounds(groups), received):
        raw_ref[comes_from(plan, my_grp, my_rep)] = ref[...]
    condition(period, raw_ref, taps_ref, white_ref)

    own = white_ref[:TILE, :LANES].astype(jnp.bfloat16)
    row = lax.broadcasted_iota(jnp.int32, (LANES, LANES), 0)
    col = lax.broadcasted_iota(jnp.int32, (LANES, LANES), 1)
    flip = jnp.where(row + col == LANES - 1, 1.0, 0.0).astype(jnp.bfloat16)
    reverse_ref[...] = dot(own, flip)
    partner = white_ref[TILE:, :].astype(jnp.bfloat16)
    rows = partner.shape[0]
    partner_ref[:rows] = partner[:, : 2 * LANES]
    partner_ref[rows:] = partner[:, LANES:]
    listed = rows // TILE
    normalizer = 1.0 / math.sqrt(LANES)
    keep = col <= row
    even, odd = (low_even, high_even), (low_odd, high_odd)
    count = TILE // 8
    parts = 4
    share = listed // parts

    def band(channel):
        line = jnp.broadcast_to(reverse_ref[pl.ds(channel, 1), :], (LANES, LANES))
        turned = pltpu.roll(line, 1, 1, stride=1, stride_axis=0)
        first = jnp.where(keep, turned, 0.0).astype(jnp.bfloat16)
        second = jnp.where(keep, 0.0, turned).astype(jnp.bfloat16)
        return jnp.concatenate([first, second], axis=0)

    def outgoing(group, part):
        tiles = pl.ds(part * share, share)
        return pltpu.make_async_copy(
            packed_ref.at[group, tiles],
            out_hbm.at[0, tiles, :, pl.ds(group * 8, 8), :],
            semaphores.at[group, part],
        )

    wide = 4

    def multiply(group, part, held):
        channel = group * 8 + wide * part
        weights = jnp.concatenate([band(channel + side) for side in range(wide)], axis=1)
        product = dot(partner_ref[...], weights)
        for half, ref in enumerate(held):
            for side in range(wide):
                ref[pl.ds(wide * part + side, rows, stride=STRIDE), :] = product[
                    half * rows : (half + 1) * rows, side * LANES : (side + 1) * LANES
                ]

    def convert(group, part, held):
        for tile in range(part * share, (part + 1) * share):
            for line in range(TILE):
                at = pl.ds((tile * TILE + line) * STRIDE, 8)
                both = jnp.concatenate([ref[at, :] for ref in held], axis=1)
                packed_ref[group, tile, line] = (both * normalizer).astype(jnp.bfloat16)

    def together(group, held, before):
        for part in range(parts):
            if part % 2 == 0:
                multiply(group, part // 2, held)
            convert(group - 1, part, before)
            outgoing(group - 1, part).start(priority=part % 2)

    for part in range(8 // wide):
        multiply(0, part, even)

    def two_groups(index, carry):
        together(2 * index + 1, odd, even)
        together(2 * index + 2, even, odd)
        return carry

    lax.fori_loop(0, count // 2, two_groups, 0)
    for part in range(parts):
        convert(count - 1, part, even)
        outgoing(count - 1, part).start(priority=part % 2)
    for group in range(count):
        for part in range(parts):
            outgoing(group, part).wait()


def correlate(received, taps, period, listed):
    groups = len(received)
    rows, packed = received[0].shape
    lines = listed * TILE
    vmem = pl.BlockSpec(memory_space=pltpu.VMEM)
    return pl.pallas_call(
        functools.partial(correlate_kernel, period),
        out_shape=jax.ShapeDtypeStruct((1, listed, TILE, TILE, LAGS), jnp.bfloat16),
        in_specs=[vmem] * (groups + 1),
        out_specs=pl.BlockSpec(memory_space=pltpu.HBM),
        scratch_shapes=[
            pltpu.VMEM((groups, rows, packed), jnp.bfloat16),
            pltpu.VMEM(((listed + 1) * TILE, groups * period), jnp.float32),
            pltpu.VMEM((2 * lines, 2 * LANES), jnp.bfloat16),
            pltpu.VMEM((TILE, LANES), jnp.float32),
        ]
        + [pltpu.VMEM((lines * STRIDE, LANES), jnp.float32)] * 4
        + [
            pltpu.VMEM((TILE // 8, listed, TILE, 8, LAGS), jnp.bfloat16),
            pltpu.SemaphoreType.DMA((TILE // 8, 4)),
        ],
        compiler_params=pltpu.CompilerParams(vmem_limit_bytes=40 * 2**20),
        name="correlate",
    )(taps, *received)


def on_device(strain, fir_taps, half_widths, pairs):
    groups = lax.axis_size("grp")
    rep_count = lax.axis_size("rep")
    *messages, taps = pack(strain, fir_taps, half_widths, pairs, groups, rep_count)
    received = []
    for plan, message in zip(rounds(groups), messages):
        if plan[0] != tuple(range(groups)):
            way = [
                (group * rep_count + member, plan[member % 2][group] * rep_count + (member ^ plan[2]))
                for group in range(groups)
                for member in range(rep_count)
            ]
            message = lax.ppermute(message, ("grp", "rep"), way)
        received.append(message)
    return correlate(received, taps, strain.shape[1], pairs.shape[1])


def solution(mesh):
    placed = (P(None, "grp"), P(), P("grp"), P())
    return jax.shard_map(
        on_device,
        mesh=mesh,
        in_specs=placed,
        out_specs=P(("grp", "rep"), None, None, None, None),
        check_vma=False,
    )
```

```python
import functools
import math

import jax
import jax.numpy as jnp
from jax import lax
from jax.experimental import pallas as pl
from jax.experimental.pallas import tpu as pltpu
from jax.sharding import PartitionSpec as P

TILE = 40
LAGS = 256
LANES = 128
STRIDE = 8
PER_BLOCK = LANES // TILE


def fetch(pairs, semaphores):
    copies = [
        pltpu.make_async_copy(source, target, semaphores.at[index])
        for index, (source, target) in enumerate(pairs)
    ]
    for copy in copies:
        copy.start()
    for copy in copies:
        copy.wait()


ROUTES = (
    ((2, 3, 4, 5, 6, 7, 0, 1), (3, 2, 5, 4, 7, 6, 1, 0), 0),
    ((2, 3, 4, 5, 6, 7, 0, 1), (5, 4, 7, 6, 1, 0, 3, 2), 1),
    ((1, 0, 3, 2, 5, 4, 7, 6), (7, 6, 1, 0, 3, 2, 5, 4), 1),
    ((4, 5, 6, 7, 0, 1, 2, 3), (7, 6, 1, 0, 3, 2, 5, 4), 0),
    ((4, 5, 6, 7, 0, 1, 2, 3), (3, 2, 5, 4, 7, 6, 1, 0), 1),
    ((1, 0, 3, 2, 5, 4, 7, 6), (5, 4, 7, 6, 1, 0, 3, 2), 0),
    ((6, 7, 0, 1, 2, 3, 4, 5), (6, 7, 0, 1, 2, 3, 4, 5), 0),
)


def rounds(groups):
    stay = tuple(range(groups))
    if groups == len(ROUTES[0][0]):
        return list(ROUTES) + [(stay, stay, 0)]
    steps = [tuple(group ^ step for group in range(groups)) for step in reversed(range(groups))]
    return [(route, route, 0) for route in steps]


def goes_to(plan, group, member):
    even, odd, _ = plan
    if even == odd:
        return pick(even, group)
    return jnp.where(lax.rem(member, 2) == 0, pick(even, group), pick(odd, group))


def comes_from(plan, group, member):
    even, odd, crossed = plan
    return goes_to((inverse(even), inverse(odd), 0), group, member ^ crossed)


def inverse(route):
    return tuple(route.index(group) for group in range(len(route)))


def pick(route, group):
    if len(route) > 8:
        return group ^ route[0]
    code = sum(target << (3 * index) for index, target in enumerate(route))
    return (jnp.int32(code) >> (3 * group)) & 7


def pack_kernel(rep_count, pairs_hbm, strain_hbm, widths_hbm, taps_hbm, *refs):
    out_refs = refs[:-7]
    taps_ref = refs[-7]
    pairs_ref, strain_ref, widths_ref, semaphores, blocks_ref, table_ref = refs[-6:]
    groups = len(out_refs)
    rows, packed = out_refs[0].shape
    listed = pairs_ref.shape[0]
    channels = strain_ref.shape[1]
    members = widths_ref.shape[1]
    fetch(
        [
            (strain_hbm, strain_ref),
            (pairs_hbm, pairs_ref),
            (widths_hbm, widths_ref),
            (taps_hbm, taps_ref),
        ],
        semaphores,
    )
    my_rep = lax.axis_index("rep")
    my_grp = lax.axis_index("grp")

    count = channels // LANES
    filled = strain_ref.shape[0]
    for block in range(count):
        values = strain_ref[:, block * LANES : (block + 1) * LANES].astype(jnp.float32)
        if rows > filled:
            values = jnp.concatenate([values, jnp.zeros((rows - filled, LANES), jnp.float32)], axis=0)
        blocks_ref[block] = values
    blocks_ref[count] = jnp.zeros((rows, LANES), jnp.float32)

    wide = jnp.concatenate(
        [widths_ref[...].astype(jnp.float32), jnp.zeros((1, 2 * LANES - members), jnp.float32)],
        axis=1,
    )
    wide = jnp.broadcast_to(wide, (TILE, 2 * LANES))
    tall = lax.broadcasted_iota(jnp.int32, (TILE, 2 * LANES), 0)
    across = lax.broadcasted_iota(jnp.int32, (TILE, 2 * LANES), 1)
    for member in range(rep_count):
        column = jnp.sum(jnp.where(across == tall + member * TILE, wide, 0.0), axis=1, keepdims=True)
        table_ref[member, :TILE] = jnp.broadcast_to(column, (TILE, LANES))
        table_ref[member, TILE:] = jnp.zeros((rows - TILE, LANES), jnp.float32)

    lane = lax.broadcasted_iota(jnp.int32, (rows, LANES), 1)
    spare = LANES - 8
    for plan, out_ref in zip(rounds(groups), out_refs):
        group = goes_to(plan, my_grp, my_rep)
        tile = group * rep_count + (my_rep ^ plan[2])
        chosen = [tile]
        member, place_of = jnp.int32(0), jnp.int32(-1)
        for slot in range(listed):
            other = pairs_ref[slot, tile]
            chosen.append(jnp.maximum(other, 0))
            among = other - my_grp * rep_count
            inside = (among >= 0) & (among < rep_count)
            member = jnp.where(inside, among, member)
            place_of = jnp.where(inside, slot + 1, place_of)
        own_at = jnp.where(group == my_grp, spare, -1)
        theirs = table_ref[member]
        mine = table_ref[my_rep]
        for block in range(packed // LANES):
            total = jnp.zeros((rows, LANES), jnp.float32)
            for place in range(PER_BLOCK):
                index = block * PER_BLOCK + place
                if index > listed:
                    continue
                start = chosen[index] * TILE
                source = start >> 7
                offset = start & (LANES - 1)
                both = jnp.where(lane >= offset, blocks_ref[source], blocks_ref[source + 1])
                shift = (place * TILE - offset) & (LANES - 1)
                moved = pltpu.roll(both, shift, 1)
                here = (lane >= place * TILE) & (lane < (place + 1) * TILE)
                total = jnp.where(here, moved, total)
            first = block * PER_BLOCK
            here = (place_of >= first) & (place_of < first + PER_BLOCK)
            marked = jnp.where(here, spare + place_of - first, -1)
            total = jnp.where(lane == marked, theirs, total)
            if block == 0:
                total = jnp.where(lane == own_at, mine, total)
            out_ref[:, block * LANES : (block + 1) * LANES] = total.astype(jnp.bfloat16)


def pack(strain, fir_taps, half_widths, pairs, groups, rep_count):
    channels, filled = strain.shape
    rows = max(filled, -(-TILE // 16) * 16)
    tiles, listed = pairs.shape
    members = half_widths.shape[0]
    packed = -(-(listed + 1) // PER_BLOCK) * LANES
    hbm = pl.BlockSpec(memory_space=pltpu.HBM)
    vmem = pl.BlockSpec(memory_space=pltpu.VMEM)
    return pl.pallas_call(
        functools.partial(pack_kernel, rep_count),
        out_shape=[jax.ShapeDtypeStruct((rows, packed), jnp.bfloat16)] * groups
        + [jax.ShapeDtypeStruct((1, fir_taps.shape[0]), jnp.float32)],
        in_specs=[hbm] * 4,
        out_specs=[vmem] * (groups + 1),
        scratch_shapes=[
            pltpu.SMEM((listed, tiles), jnp.int32),
            pltpu.VMEM((filled, channels), jnp.bfloat16),
            pltpu.VMEM((1, members), jnp.int32),
            pltpu.SemaphoreType.DMA((4,)),
            pltpu.VMEM((channels // LANES + 1, rows, LANES), jnp.float32),
            pltpu.VMEM((rep_count, rows, LANES), jnp.float32),
        ],
        compiler_params=pltpu.CompilerParams(vmem_limit_bytes=48 * 2**20),
        name="pack",
    )(*[
        pltpu.with_memory_space_constraint(array, pltpu.HBM)
        for array in (pairs.T, strain.T, half_widths[None, :], fir_taps[None, :])
    ])


def split(values):
    high = values.astype(jnp.bfloat16)
    low = (values - high.astype(jnp.float32)).astype(jnp.bfloat16)
    return high, low


def dot(left, right):
    return jnp.dot(left, right, preferred_element_type=jnp.float32)


def condition(period, raw_ref, taps_ref, white_ref):
    groups, rows, packed = raw_ref.shape
    listed = white_ref.shape[0] // TILE - 1
    blocks = packed // LANES
    raw = raw_ref[:, :period, :].astype(jnp.float32).reshape(groups * period, packed)
    samples = jnp.transpose(raw).astype(jnp.bfloat16)
    columns = []
    for block in range(blocks):
        piece = raw_ref[:, :TILE, block * LANES : (block + 1) * LANES].astype(jnp.float32)
        columns.append(jnp.sum(piece, axis=0))

    count = taps_ref.shape[1]
    taps = jnp.concatenate([taps_ref[...], jnp.zeros((1, 2 * LANES - count), jnp.float32)], axis=1)
    bands = pltpu.roll(jnp.broadcast_to(taps, (LANES, 2 * LANES)), 0, 1, stride=1, stride_axis=0)
    parts = []
    empty = jnp.zeros((LANES, LANES), jnp.bfloat16)
    for piece in split(bands):
        near, far = piece[:, :LANES], piece[:, LANES:]
        first = jnp.concatenate([piece, jnp.concatenate([empty, near], axis=1)], axis=0)
        second = jnp.concatenate([far, near], axis=0)
        parts.append((dot(samples[:, : 2 * LANES], first), dot(samples[:, LANES:], second)))
    filtered = jnp.concatenate([parts[0][0] + parts[1][0], parts[0][1] + parts[1][1]], axis=1)

    size = jnp.abs(filtered)
    before = lax.broadcasted_iota(jnp.int32, (2 * LANES, 2 * LANES), 0) <= lax.broadcasted_iota(
        jnp.int32, (2 * LANES, 2 * LANES), 1
    )
    upper = jnp.where(before, 1.0, 0.0).astype(jnp.bfloat16)
    ones = jnp.ones((2 * LANES, LANES), jnp.bfloat16)
    sums = []
    for piece in split(size):
        head, tail = piece[:, : 2 * LANES], piece[:, 2 * LANES :]
        sums.append((dot(head, upper), dot(head, ones), dot(tail, upper[:LANES, :LANES])))
    high, low = sums
    head = high[0] + low[0]
    tail = (high[1] + low[1]) + (high[2] + low[2])
    prefix = [head[:, :LANES], head[:, LANES:], tail]

    lane = lax.broadcasted_iota(jnp.int32, (TILE, LANES), 1)
    for slot in range(listed + 1):
        base = slot // PER_BLOCK * LANES + slot % PER_BLOCK * TILE
        at = slice(base, base + TILE)
        from_lane = LANES - 8 + slot % PER_BLOCK
        column = columns[slot // PER_BLOCK][:, from_lane : from_lane + 1]
        width = jnp.broadcast_to(column, (TILE, LANES))
        whole = width.astype(jnp.int32)
        above = lane + whole
        below = lane - whole - 1
        above_at = above & (LANES - 1)
        below_at = below & (LANES - 1)
        above_by = above >> 7
        below_by = below >> 7
        up = [jnp.take_along_axis(prefix[b][at], above_at, axis=1) for b in range(3)]
        down = [jnp.take_along_axis(prefix[b][at], below_at, axis=1) for b in range(2)]
        full = jnp.broadcast_to(prefix[2][at][:, LANES - 1 :], (TILE, LANES))
        ends = up + [full, full]
        starts = [jnp.zeros((TILE, LANES), jnp.float32)] * 2 + down
        down_last = jnp.take_along_axis(prefix[2][at], below_at, axis=1)
        starts.append(down_last)
        scale = 1.0 / (2.0 * width + 1.0)
        high_0, high_1 = above_by == 0, above_by == 1
        low_0, low_1 = below_by == 0, below_by == -1
        for block in range(3 if slot else 1):
            top = jnp.where(high_0, ends[block], jnp.where(high_1, ends[block + 1], ends[block + 2]))
            low_end = jnp.where(
                low_0, starts[block + 2], jnp.where(low_1, starts[block + 1], starts[block])
            )
            level = (top - low_end) * scale
            value = filtered[at, block * LANES : (block + 1) * LANES] / (level + 1e-05)
            if slot:
                value = jnp.where(width > 0.0, value, 0.0)
            white_ref[slot * TILE : (slot + 1) * TILE, block * LANES : (block + 1) * LANES] = value


def correlate_kernel(period, taps_ref, *refs):
    received = refs[:-11]
    out_hbm, raw_ref, white_ref, partner_ref, reverse_ref = refs[-11:-6]
    low_even, high_even, low_odd, high_odd, packed_ref, semaphores = refs[-6:]
    groups = len(received)
    my_grp = lax.axis_index("grp")
    my_rep = lax.axis_index("rep")
    for plan, ref in zip(rounds(groups), received):
        raw_ref[comes_from(plan, my_grp, my_rep)] = ref[...]
    condition(period, raw_ref, taps_ref, white_ref)

    own = white_ref[:TILE, :LANES].astype(jnp.bfloat16)
    row = lax.broadcasted_iota(jnp.int32, (LANES, LANES), 0)
    col = lax.broadcasted_iota(jnp.int32, (LANES, LANES), 1)
    flip = jnp.where(row + col == LANES - 1, 1.0, 0.0).astype(jnp.bfloat16)
    reverse_ref[...] = dot(own, flip)
    partner = white_ref[TILE:, :].astype(jnp.bfloat16)
    rows = partner.shape[0]
    partner_ref[:rows] = partner[:, : 2 * LANES]
    partner_ref[rows:] = partner[:, LANES:]
    listed = rows // TILE
    normalizer = 1.0 / math.sqrt(LANES)
    keep = col <= row
    even, odd = (low_even, high_even), (low_odd, high_odd)
    count = TILE // 8
    parts = 4
    share = listed // parts

    def band(channel):
        line = jnp.broadcast_to(reverse_ref[pl.ds(channel, 1), :], (LANES, LANES))
        turned = pltpu.roll(line, 1, 1, stride=1, stride_axis=0)
        first = jnp.where(keep, turned, 0.0).astype(jnp.bfloat16)
        second = jnp.where(keep, 0.0, turned).astype(jnp.bfloat16)
        return jnp.concatenate([first, second], axis=0)

    def outgoing(group, part):
        tiles = pl.ds(part * share, share)
        return pltpu.make_async_copy(
            packed_ref.at[group, tiles],
            out_hbm.at[0, tiles, :, pl.ds(group * 8, 8), :],
            semaphores.at[group, part],
        )

    wide = 4

    def multiply(group, part, held):
        channel = group * 8 + wide * part
        weights = jnp.concatenate([band(channel + side) for side in range(wide)], axis=1)
        product = dot(partner_ref[...], weights) * normalizer
        for half, ref in enumerate(held):
            for side in range(wide):
                ref[pl.ds(wide * part + side, rows, stride=STRIDE), :] = product[
                    half * rows : (half + 1) * rows, side * LANES : (side + 1) * LANES
                ]

    def convert(group, part, held):
        for tile in range(part * share, (part + 1) * share):
            for line in range(TILE):
                at = pl.ds((tile * TILE + line) * STRIDE, 8)
                both = jnp.concatenate([ref[at, :] for ref in held], axis=1)
                packed_ref[group, tile, line] = both.astype(jnp.bfloat16)

    def together(group, held, before):
        for part in range(parts):
            if part % 2 == 0:
                multiply(group, part // 2, held)
            convert(group - 1, part, before)
            outgoing(group - 1, part).start(priority=part % 2)

    for part in range(8 // wide):
        multiply(0, part, even)

    def two_groups(index, carry):
        together(2 * index + 1, odd, even)
        together(2 * index + 2, even, odd)
        return carry

    lax.fori_loop(0, count // 2, two_groups, 0)
    for part in range(parts):
        convert(count - 1, part, even)
        outgoing(count - 1, part).start(priority=part % 2)
    for group in range(count):
        for part in range(parts):
            outgoing(group, part).wait()


def correlate(received, taps, period, listed):
    groups = len(received)
    rows, packed = received[0].shape
    lines = listed * TILE
    vmem = pl.BlockSpec(memory_space=pltpu.VMEM)
    return pl.pallas_call(
        functools.partial(correlate_kernel, period),
        out_shape=jax.ShapeDtypeStruct((1, listed, TILE, TILE, LAGS), jnp.bfloat16),
        in_specs=[vmem] * (groups + 1),
        out_specs=pl.BlockSpec(memory_space=pltpu.HBM),
        scratch_shapes=[
            pltpu.VMEM((groups, rows, packed), jnp.bfloat16),
            pltpu.VMEM(((listed + 1) * TILE, groups * period), jnp.float32),
            pltpu.VMEM((2 * lines, 2 * LANES), jnp.bfloat16),
            pltpu.VMEM((TILE, LANES), jnp.float32),
        ]
        + [pltpu.VMEM((lines * STRIDE, LANES), jnp.float32)] * 4
        + [
            pltpu.VMEM((TILE // 8, listed, TILE, 8, LAGS), jnp.bfloat16),
            pltpu.SemaphoreType.DMA((TILE // 8, 4)),
        ],
        compiler_params=pltpu.CompilerParams(vmem_limit_bytes=40 * 2**20),
        name="correlate",
    )(taps, *received)


def on_device(strain, fir_taps, half_widths, pairs):
    groups = lax.axis_size("grp")
    rep_count = lax.axis_size("rep")
    *messages, taps = pack(strain, fir_taps, half_widths, pairs, groups, rep_count)
    received = []
    for plan, message in zip(rounds(groups), messages):
        if plan[0] != tuple(range(groups)):
            way = [
                (group * rep_count + member, plan[member % 2][group] * rep_count + (member ^ plan[2]))
                for group in range(groups)
                for member in range(rep_count)
            ]
            message = lax.ppermute(message, ("grp", "rep"), way)
        received.append(message)
    return correlate(received, taps, strain.shape[1], pairs.shape[1])


def solution(mesh):
    placed = (P(None, "grp"), P(), P("grp"), P())
    return jax.shard_map(
        on_device,
        mesh=mesh,
        in_specs=placed,
        out_specs=P(("grp", "rep"), None, None, None, None),
        check_vma=False,
    )
```
